256 devices in a mesh: view: 64 (over x, z, core), pix: 4 (over y).
Axes of the slice: x: 4, y: 4, z: 8, core: 2. Of those that a mesh axis runs over, the one named last changes fastest.
Arguments:
- target_tokens: bfloat16 [32768, 1024], P(('view', 'pix')), may hold values from -6 to 6
- input_tokens: bfloat16 [32768, 1024], P(('view', 'pix')), may hold values from -6 to 6
- w_query: bfloat16 [1024, 1024], P(None, 'pix')
- w_key: bfloat16 [1024, 1024], P(None, 'pix'), may hold values from -0.1875 to 0.1875
- w_value: bfloat16 [1024, 1024], P(None, 'pix'), may hold values from -0.1875 to 0.1875
- w_out: bfloat16 [1024, 1024], P('pix'), may hold values from -0.75 to 0.75
- table: int32 [256, 8], replicated, may hold values from 0 to 63, all different within a row; in each aligned block of 4 rows (0 to 3, 4 to 7, ...) at most 2 rows name the same one
- table_block: int32 [256, 8], replicated, may hold values from 0 to 3
- counts: int32 [256], P('view'), may hold values from 1 to 8
Outputs:
- output: bfloat16 [32768, 1024], P(('view', 'pix'))
The draws below stay inside these ranges and needn't reach their ends.
Inputs may be any that keep to these rules, and one draw needn't show every extreme that they name: `table`: the entries of one row name different input views; within the rows of one target view (aligned blocks of 4 rows) no input view is named by more than 2 entries, counting all 8 columns.
All inputs are finite; a program needn't handle non-finite values.
Results may differ from the reference program's by a relative error of at most 0.0095.
The reference program's roundings to bfloat16 on the way count: a program that leaves them out, or rounds other values in their place, can miss the bound.
Values may be sent and summed in bfloat16 or wider, within the bound.
A program may use at most 128 MiB of HBM per device.

```python
import math
import jax
import jax.numpy as jnp
import numpy as np
from jax import lax

D = 1024
HEADS = 16
HEAD_DIM = 64
VIEW_TOK = 512
BLOCK = 128
VIEWS = 64
VIEW_BLOCKS = 4
TBLOCKS = 256
LIST_LEN = 8
CAP = 2


def draw_w_query(key, part):
    key = jax.random.fold_in(key, 5)
    base_key = jax.random.fold_in(key, 1)
    spread = (D // 4) ** (-0.5)
    base = jax.random.normal(base_key, (D, D), jnp.float32) * spread
    return base.astype(jnp.bfloat16)


def plant(array, stream_key, least, high):
    shape = array.shape
    index_at = [jax.random.randint(jax.random.fold_in(stream_key, axis), (), 0, shape[axis]) for axis in range(len(shape))]
    array = array.at[tuple(index_at)].set(least)
    longest = shape.index(max(shape))
    index_at[longest] = (index_at[longest] + 1) % shape[longest]
    return array.at[tuple(index_at)].set(high)


def block_scale(stream_key, dims, cuts, low, high):
    factor_of, own = 1.0, jax.random.fold_in(stream_key, 6)
    for axis_at, shards_of in cuts:
        steps = jnp.exp(jax.random.uniform(jax.random.fold_in(own, axis_at), (shards_of,), jnp.float32, low / len(cuts), high / len(cuts)))
        factor_of = factor_of * jnp.repeat(steps, dims[axis_at] // shards_of).reshape([-1 if axis == axis_at else 1 for axis in range(len(dims))])
    return factor_of


def routed_block(stream_key, own, number, rows, amount, top, most, skew):
    ranking = jax.random.permutation(stream_key, amount)
    crowded, ordinary = shares(amount, rows * top, most, skew, True), shares(amount, rows * top, most, skew, False)
    places = jnp.arange(amount)

    def named(lengths, offset_by):
        used = int((lengths > 0).sum())
        fixed = max(1, used // 4)
        shifted = fixed + (places - fixed + offset_by * (used - fixed)) % max(1, amount - fixed)
        return jnp.zeros((amount,), jnp.int32).at[ranking[jnp.where(places < fixed, places, shifted)]].set(jnp.asarray(lengths, jnp.int32))

    lengths = jnp.where(number % 4 == 0, named(crowded, number // 4), named(ordinary, number - number // 4 - 1))
    mixed = jax.random.permutation(jax.random.fold_in(own, 3), amount)
    giver, taker = mixed[0:amount // 2 * 2:2], mixed[1:amount // 2 * 2:2]
    margin = jnp.minimum(lengths[giver] - 1, most - lengths[taker]) // 2
    margin = jnp.where((giver == ranking[0]) | (taker == ranking[0]) | (lengths[taker] == 0), 0, jnp.maximum(margin, 0))
    shifted = jax.random.randint(jax.random.fold_in(own, 4), (amount // 2,), 0, 1 << 20) % (margin + 1)
    lengths = lengths.at[giver].add(-shifted).at[taker].add(shifted)
    members = jnp.searchsorted(jnp.cumsum(lengths), jnp.arange(rows * top), side="right").astype(jnp.int32)
    grid = members.reshape(top, rows).T
    grid = grid[jax.random.permutation(jax.random.fold_in(own, 1), rows)]
    offset_by = jax.random.randint(jax.random.fold_in(own, 2), (rows, 1), 0, top)
    return jnp.take_along_axis(grid, (jnp.arange(top)[None, :] + offset_by) % top, axis=1)


def shares(count, total, most, slope, full):
    loads = [(1 << 20) // math.isqrt(grade ** slope) + 1 for grade in range(1, count + 1)]
    largest = most if full else min(most, max(-(-total // count), total * loads[0] // sum(loads)))
    least = 1 if total - largest >= count - 1 else 0
    holding, spare = [largest] + [least] * (count - 1), total - largest - least * (count - 1)
    while spare > 0:
        candidates = [i for i in range(1, count) if holding[i] < largest] or [i for i in range(1, count) if holding[i] < most]
        mass, remaining = sum([loads[i] for i in candidates]), spare
        for i in candidates:
            more = min(most - holding[i], max(1, remaining * loads[i] // mass), spare)
            holding[i] = holding[i] + more
            spare = spare - more
    return np.array(holding)


def normal_values(key, extent, scale, most, split=(), kind=jnp.bfloat16):
    result = scale * jax.random.normal(key, extent, jnp.float32)
    if split:
        result = result * block_scale(key, extent, split, -0.22, 0.18)
    return jnp.clip(result, -most, most).astype(kind)


def setup_inputs(seed: int = 0) -> dict:
    arg_keys = jax.random.split(jax.random.key(seed), 10)
    target_tokens = normal_values(arg_keys[0], (VIEWS * VIEW_TOK, D), 1.0, 6.0, ((0, 256),))
    input_tokens = normal_values(arg_keys[1], (VIEWS * VIEW_TOK, D), 1.0, 6.0, ((0, 256),))
    w_query = draw_w_query(jax.random.fold_in(arg_keys[9], 71), 0)
    w_key = normal_values(arg_keys[3], (D, D), D ** -0.5, 0.1875, ((1, 4),))
    w_value = normal_values(arg_keys[4], (D, D), D ** -0.5, 0.1875, ((1, 4),))
    w_out = normal_values(arg_keys[5], (D, D), (D // 16) ** -0.5, 0.75, ((0, 4),))
    table_keys = jax.random.split(jax.random.fold_in(arg_keys[6], 1), TBLOCKS // VIEW_BLOCKS)
    table_turns = jax.random.permutation(jax.random.fold_in(arg_keys[6], 3), TBLOCKS // VIEW_BLOCKS)
    table = jax.vmap(lambda own, number: routed_block(jax.random.fold_in(arg_keys[6], 2), own, number, VIEW_BLOCKS, VIEWS, LIST_LEN, CAP, 2))(table_keys, table_turns).reshape((TBLOCKS, LIST_LEN))
    table_block = plant(jax.random.randint(arg_keys[7], (TBLOCKS, LIST_LEN), 0, VIEW_BLOCKS), jax.random.fold_in(arg_keys[7], 1), 0, VIEW_BLOCKS - 1).astype(jnp.int32)
    counts = plant(jax.random.randint(arg_keys[8], (TBLOCKS,), 1, LIST_LEN + 1), jax.random.fold_in(arg_keys[8], 1), 1, LIST_LEN).astype(jnp.int32)
    return dict(target_tokens=target_tokens, input_tokens=input_tokens, w_query=w_query, w_key=w_key, w_value=w_value, w_out=w_out, table=table, table_block=table_block, counts=counts)


def normalize(tokens):
    source = tokens.astype(jnp.float32)
    center = source - lax.optimization_barrier(jnp.mean(source, axis=1, keepdims=True))
    spread = lax.optimization_barrier(jnp.mean(center * center, axis=1, keepdims=True))
    return (center * lax.rsqrt(spread + 1e-05)).astype(jnp.bfloat16)

def reference(target_tokens, input_tokens, w_query, w_key, w_value, w_out, table, table_block, counts):
    normed_target = normalize(target_tokens)
    normed_input = normalize(input_tokens)
    queries = jnp.dot(normed_target, w_query, preferred_element_type=jnp.float32).astype(jnp.bfloat16)
    keys_all = jnp.dot(normed_input, w_key, preferred_element_type=jnp.float32).astype(jnp.bfloat16)
    values_all = jnp.dot(normed_input, w_value, preferred_element_type=jnp.float32).astype(jnp.bfloat16)
    key_blocks = keys_all.reshape(VIEWS * VIEW_BLOCKS, BLOCK, HEADS, HEAD_DIM)
    value_blocks = values_all.reshape(VIEWS * VIEW_BLOCKS, BLOCK, HEADS, HEAD_DIM)
    entry_ids = (table * VIEW_BLOCKS + table_block).astype(jnp.int32)
    query_blocks = queries.reshape(TBLOCKS, BLOCK, HEADS, HEAD_DIM)
    scale = HEAD_DIM ** (-0.5)

    def one_block(packed):
        query_block, ids, valid = packed
        key_rows = jnp.take(key_blocks, ids, axis=0).reshape(LIST_LEN * BLOCK, HEADS, HEAD_DIM)
        value_rows = jnp.take(value_blocks, ids, axis=0).reshape(LIST_LEN * BLOCK, HEADS, HEAD_DIM)
        scores = jnp.einsum('qhd,khd->hqk', query_block.astype(jnp.float32), key_rows.astype(jnp.float32)) * scale
        live = jnp.arange(LIST_LEN * BLOCK, dtype=jnp.int32) // BLOCK < valid
        scores = jnp.where(live[None, None, :], scores, -1e+30)
        peak = lax.optimization_barrier(jnp.max(scores, axis=2, keepdims=True))
        weights = jnp.exp(scores - peak)
        probs = (weights / lax.optimization_barrier(jnp.sum(weights, axis=2, keepdims=True))).astype(jnp.bfloat16)
        attended = jnp.einsum('hqk,khd->qhd', probs.astype(jnp.float32), value_rows.astype(jnp.float32))
        return attended.astype(jnp.bfloat16).reshape(BLOCK, HEADS * HEAD_DIM)
    attended = lax.map(one_block, (query_blocks, entry_ids, counts)).reshape(TBLOCKS * BLOCK, HEADS * HEAD_DIM)
    mixed = jnp.dot(attended, w_out, preferred_element_type=jnp.float32)
    return (target_tokens.astype(jnp.float32) + mixed).astype(jnp.bfloat16)
```

```python
import jax
import jax.numpy as jnp
from jax import lax
from jax.experimental import pallas as pl
from jax.experimental.pallas import tpu as pltpu
from jax.sharding import Mesh, PartitionSpec as P

D = 1024
HEAD_DIM = 64
BLOCK = 128
LIST_LEN = 8
PIX = 4
GROUP = ("x", "core", "pix")


def normalize(tokens):
    source = tokens.astype(jnp.float32)
    center = source - jnp.mean(source, axis=1, keepdims=True)
    spread = jnp.mean(center * center, axis=1, keepdims=True)
    return (center * lax.rsqrt(spread + 1e-05)).astype(jnp.bfloat16)


def attend_kernel(count_ref, target_ref, listed_ref, wq_ref, wk_ref, wv_ref, wo_ref, out_ref, normed, total):
    step = pl.program_id(0)

    @pl.when(step == 0)
    def _():
        normed[...] = normalize(target_ref[...])

    listed = listed_ref[...]
    query = jnp.dot(normed[...], wq_ref[0], preferred_element_type=jnp.float32).astype(jnp.bfloat16)
    key = jnp.dot(listed, wk_ref[0], preferred_element_type=jnp.float32).astype(jnp.bfloat16)
    value = jnp.dot(listed, wv_ref[0], preferred_element_type=jnp.float32).astype(jnp.bfloat16)
    columns = lax.broadcasted_iota(jnp.int32, (1, LIST_LEN * BLOCK), 1)
    live = columns < count_ref[0] * BLOCK
    heads = []
    for h in range(query.shape[1] // HEAD_DIM):
        part = slice(h * HEAD_DIM, (h + 1) * HEAD_DIM)
        scores = lax.dot_general(
            query[:, part], key[:, part], (((1,), (1,)), ((), ())), preferred_element_type=jnp.float32
        )
        scores = jnp.where(live, scores * HEAD_DIM ** (-0.5), -1e30)
        peak = jnp.max(scores, axis=1, keepdims=True)
        weights = jnp.exp(scores - peak)
        probs = (weights * (1.0 / jnp.sum(weights, axis=1, keepdims=True))).astype(jnp.bfloat16)
        heads.append(jnp.dot(probs, value[:, part], preferred_element_type=jnp.float32).astype(jnp.bfloat16))
    attended = jnp.concatenate(heads, axis=1)
    mixed = jnp.dot(attended, wo_ref[0], preferred_element_type=jnp.float32)

    @pl.when(step == 0)
    def _():
        total[...] = mixed

    @pl.when(step > 0)
    def _():
        total[...] += mixed

    @pl.when(step == pl.num_programs(0) - 1)
    def _():
        out_ref[...] = (target_ref[...].astype(jnp.float32) + total[...]).astype(jnp.bfloat16)


def attend(count, target, listed, wq, wk, wv, wo):
    cols = D // PIX
    whole = lambda shape: pl.BlockSpec(shape, lambda i: (0, 0))
    return pl.pallas_call(
        attend_kernel,
        grid=(PIX,),
        out_shape=jax.ShapeDtypeStruct((BLOCK, D), jnp.bfloat16),
        in_specs=[
            pl.BlockSpec(memory_space=pltpu.SMEM),
            whole((BLOCK, D)),
            whole((LIST_LEN * BLOCK, D)),
            pl.BlockSpec((1, D, cols), lambda i: (i, 0, 0)),
            pl.BlockSpec((1, D, cols), lambda i: (i, 0, 0)),
            pl.BlockSpec((1, D, cols), lambda i: (i, 0, 0)),
            pl.BlockSpec((1, cols, D), lambda i: (i, 0, 0)),
        ],
        out_specs=whole((BLOCK, D)),
        scratch_shapes=[pltpu.VMEM((BLOCK, D), jnp.bfloat16), pltpu.VMEM((BLOCK, D), jnp.float32)],
        compiler_params=pltpu.CompilerParams(vmem_limit_bytes=48 * 1024 * 1024),
        cost_estimate=pl.CostEstimate(flops=5_400_000_000, bytes_accessed=11 << 20, transcendentals=2 << 20),
    )(count, target, listed, wq, wk, wv, wo)


def body(target_tokens, input_tokens, w_query, w_key, w_value, w_out, table, table_block, counts):
    x, z, core, y = (lax.axis_index(name) for name in ("x", "z", "core", "pix"))
    nx, nz, nc = (lax.axis_size(name) for name in ("x", "z", "core"))
    members = nx * nc * PIX
    normed = normalize(input_tokens)
    pieces = normed.reshape(nx * nc, 16, PIX, D // PIX).transpose(0, 2, 1, 3).reshape(members, 16, D // PIX)
    spread = lax.all_to_all(pieces, GROUP, split_axis=0, concat_axis=0, tiled=True)
    held = lax.all_gather(spread, "z", axis=0, tiled=True)
    weights = [lax.all_gather(w, "pix", axis=0, tiled=False) for w in (w_query, w_key, w_value, w_out)]
    place = ((table // 2) % nz) * members + ((table // (2 * nz)) * nc + table % nc) * PIX + table_block
    place = place.reshape(nx, nz, nc * PIX, LIST_LEN)
    wanted = lax.dynamic_index_in_dim(place, z, 1, keepdims=False).reshape(-1)
    outgoing = jnp.take(held, wanted, axis=0).reshape(members, LIST_LEN, 16, D // PIX)
    arrived = lax.all_to_all(outgoing, GROUP, split_axis=0, concat_axis=0, tiled=True)
    listed = arrived.reshape(nx * nc, PIX, LIST_LEN, 16, D // PIX).transpose(2, 0, 3, 1, 4)
    listed = listed.reshape(LIST_LEN * BLOCK, D)
    count = lax.dynamic_slice_in_dim(counts, y, 1, 0)
    return attend(count, target_tokens, listed, *weights)


def solution(mesh):
    views = ("x", "z", "core")
    fine = Mesh(mesh.devices.reshape(4, 8, 2, 4), ("x", "z", "core", "pix"))
    placed = (
        P((*views, "pix"), None),
        P((*views, "pix"), None),
        P(None, "pix"),
        P(None, "pix"),
        P(None, "pix"),
        P("pix", None),
        P(),
        P(),
        P(views),
    )
    return jax.shard_map(
        body, mesh=fine, in_specs=placed, out_specs=P((*views, "pix"), None), check_vma=False
    )
```

```python
import jax
import jax.numpy as jnp
from jax import lax
from jax.experimental import pallas as pl
from jax.experimental.pallas import tpu as pltpu
from jax.sharding import Mesh, PartitionSpec as P

D = 1024
HEAD_DIM = 64
BLOCK = 128
LIST_LEN = 8
PIX = 4


def normalize(tokens):
    source = tokens.astype(jnp.float32)
    center = source - jnp.mean(source, axis=1, keepdims=True)
    spread = jnp.mean(center * center, axis=1, keepdims=True)
    return (center * lax.rsqrt(spread + 1e-05)).astype(jnp.bfloat16)


def attend_kernel(count_ref, target_ref, listed_ref, wq_ref, wk_ref, wv_ref, wo_ref, out_ref, normed, total):
    step = pl.program_id(0)

    @pl.when(step == 0)
    def _():
        normed[...] = normalize(target_ref[...])

    listed = listed_ref[...]
    query = jnp.dot(normed[...], wq_ref[0], preferred_element_type=jnp.float32).astype(jnp.bfloat16)
    key = jnp.dot(listed, wk_ref[0], preferred_element_type=jnp.float32).astype(jnp.bfloat16)
    value = jnp.dot(listed, wv_ref[0], preferred_element_type=jnp.float32).astype(jnp.bfloat16)
    columns = lax.broadcasted_iota(jnp.int32, (1, LIST_LEN * BLOCK), 1)
    live = columns < count_ref[0] * BLOCK
    heads = []
    for h in range(query.shape[1] // HEAD_DIM):
        part = slice(h * HEAD_DIM, (h + 1) * HEAD_DIM)
        scores = lax.dot_general(
            query[:, part], key[:, part], (((1,), (1,)), ((), ())), preferred_element_type=jnp.float32
        )
        scores = jnp.where(live, scores * HEAD_DIM ** (-0.5), -1e30)
        peak = jnp.max(scores, axis=1, keepdims=True)
        weights = jnp.exp(scores - peak)
        probs = (weights * (1.0 / jnp.sum(weights, axis=1, keepdims=True))).astype(jnp.bfloat16)
        heads.append(jnp.dot(probs, value[:, part], preferred_element_type=jnp.float32).astype(jnp.bfloat16))
    attended = jnp.concatenate(heads, axis=1)
    mixed = jnp.dot(attended, wo_ref[0], preferred_element_type=jnp.float32)

    @pl.when(step == 0)
    def _():
        total[...] = mixed

    @pl.when(step > 0)
    def _():
        total[...] += mixed

    @pl.when(step == pl.num_programs(0) - 1)
    def _():
        out_ref[...] = (target_ref[...].astype(jnp.float32) + total[...]).astype(jnp.bfloat16)


def attend(count, target, listed, wq, wk, wv, wo):
    cols = D // PIX
    whole = lambda shape: pl.BlockSpec(shape, lambda i: (0, 0))
    return pl.pallas_call(
        attend_kernel,
        grid=(PIX,),
        out_shape=jax.ShapeDtypeStruct((BLOCK, D), jnp.bfloat16),
        in_specs=[
            pl.BlockSpec(memory_space=pltpu.SMEM),
            whole((BLOCK, D)),
            whole((LIST_LEN * BLOCK, D)),
            pl.BlockSpec((1, D, cols), lambda i: (i, 0, 0)),
            pl.BlockSpec((1, D, cols), lambda i: (i, 0, 0)),
            pl.BlockSpec((1, D, cols), lambda i: (i, 0, 0)),
            pl.BlockSpec((1, cols, D), lambda i: (i, 0, 0)),
        ],
        out_specs=whole((BLOCK, D)),
        scratch_shapes=[pltpu.VMEM((BLOCK, D), jnp.bfloat16), pltpu.VMEM((BLOCK, D), jnp.float32)],
        compiler_params=pltpu.CompilerParams(vmem_limit_bytes=48 * 1024 * 1024),
        cost_estimate=pl.CostEstimate(flops=5_400_000_000, bytes_accessed=11 << 20, transcendentals=2 << 20),
    )(count, target, listed, wq, wk, wv, wo)


def comm_kernel(
    wanted_ref, tokens_ref, wq_ref, wk_ref, wv_ref, wo_ref,
    listed, wq, wk, wv, wo,
    pieces, held, outgoing,
    pre_send, pre_recv, ring_send, ring_recv, out_send, out_recv,
    row_send, row_recv, col_send, col_recv, pair_send, pair_recv, own_sem,
):
    x, z, core, y = (lax.axis_index(name) for name in ("x", "z", "core", "pix"))
    nx, nz, nc, ny = (lax.axis_size(name) for name in ("x", "z", "core", "pix"))
    members = nx * nc * ny
    me = (x * nc + core) * ny + y
    part = members // nx

    def member(t):
        return (t // (nc * ny), z, (t // ny) % nc, t % ny)

    up_z, down_z = (x, (z + 1) % nz, core, y), (x, (z + nz - 1) % nz, core, y)
    up_y, down_y = (x, z, core, (y + 1) % ny), (x, z, core, (y + ny - 1) % ny)
    up_x, down_x = ((x + 1) % nx, z, core, y), ((x + nx - 1) % nx, z, core, y)
    other = (x, z, 1 - core, y)

    def remote(src, dst, send, recv, device):
        return pltpu.make_async_remote_copy(
            src_ref=src, dst_ref=dst, send_sem=send, recv_sem=recv,
            device_id=device, device_id_type=pl.DeviceIdType.MESH,
        )

    barrier = pltpu.get_barrier_semaphore()

    def greet(k, carry):
        pl.semaphore_signal(
            barrier, inc=1, device_id=member((me + k) % members), device_id_type=pl.DeviceIdType.MESH
        )
        return carry

    lax.fori_loop(1, members, greet, 0)
    for device in (up_z, down_z):
        pl.semaphore_signal(barrier, inc=1, device_id=device, device_id_type=pl.DeviceIdType.MESH)

    mine = [
        pltpu.make_async_copy(src, dst.at[y], own_sem.at[i])
        for i, (src, dst) in enumerate(((wq_ref, wq), (wk_ref, wk), (wv_ref, wv), (wo_ref, wo)))
    ]
    for copy in mine:
        copy.start()
    normed = normalize(tokens_ref[...])
    for row in range(members // ny):
        for col in range(ny):
            pieces[row * ny + col] = normed[row * 16:(row + 1) * 16, col * 256:(col + 1) * 256]
    held[z * members + me] = pieces[me]
    pl.semaphore_wait(barrier, members - 1 + 2)

    def pre(t, s):
        return remote(pieces.at[t], held.at[z * members + s], pre_send.at[t], pre_recv.at[s], member(t))

    def pre_start(k, carry):
        pre((me + k) % members, me).start()
        return carry

    lax.fori_loop(1, members, pre_start, 0)

    class Ring:
        def __init__(self, own, slot, at, up, down, send, recv, base):
            self.own, self.slot, self.at, self.up, self.down = own, slot, at, up, down
            self.send, self.recv, self.base = send, recv, base

        def copy(self, i, origin, half, device, src=None):
            dst = self.slot(origin, half)
            return remote(
                dst if src is None else src, dst, self.send.at[self.base + i], self.recv.at[self.base + i], device
            )

        def begin(self):
            for half in (0, 1):
                self.copy(half, self.at, half, self.up, self.own(half)).start()
                self.copy(3 + half, self.at, half, self.down, self.own(half)).start()

        def forward(self):
            before, after = (self.at + 3) % 4, (self.at + 1) % 4
            self.copy(0, before, 0, self.up).wait_recv()
            self.copy(2, before, 0, self.up).start()
            self.copy(4, after, 1, self.down).wait_recv()
            self.copy(5, after, 1, self.down).start()

        def end(self):
            before, after, far = (self.at + 3) % 4, (self.at + 1) % 4, (self.at + 2) % 4
            self.copy(1, before, 1, self.up).wait_recv()
            self.copy(3, after, 0, self.down).wait_recv()
            self.copy(2, far, 0, self.up).wait_recv()
            self.copy(5, far, 1, self.down).wait_recv()

        def sent(self):
            for i in range(6):
                self.copy(i, self.at, i % 2, self.up).wait_send()

    def y_ring(src, dst, start, size, base):
        return Ring(
            lambda half: src.at[pl.ds(start + half * size, size)],
            lambda origin, half: dst.at[origin, pl.ds(start + half * size, size)],
            y, up_y, down_y, row_send, row_recv, base,
        )

    def x_ring(dst, quarter, first, size, base):
        def slot(origin, half):
            return dst.at[quarter, pl.ds(pl.multiple_of(first + origin * 2 * size + half * size, size), size)]

        return Ring(lambda half: slot(x, half), slot, x, up_x, down_x, col_send, col_recv, base)

    narrow = [
        y_ring(wv_ref, wv, pl.multiple_of(core * 512 + x * 128, 128), 64, 0),
        y_ring(wo_ref, wo, pl.multiple_of(core * 128 + x * 32, 32), 16, 6),
    ]
    wide = [
        y_ring(wk_ref, wk, pl.multiple_of(core * 512, 512), 256, 12),
        y_ring(wq_ref, wq, pl.multiple_of(core * 512, 512), 256, 18),
    ]
    across = [
        x_ring(dst, (y + 1 + i) % ny, pl.multiple_of(core * 8 * size, 8 * size), size, (3 * kind + i) * 6)
        for kind, (dst, size) in enumerate(((wv, 64), (wo, 16)))
        for i in range(3)
    ]

    def pair(kind, i):
        dst, rows = ((wk, 512), (wq, 512), (wv, 512), (wo, 128))[kind]
        ref = dst.at[(y + 1 + i) % ny, pl.ds(pl.multiple_of(core * rows, rows), rows)]
        return remote(ref, ref, pair_send.at[kind * 3 + i], pair_recv.at[kind * 3 + i], other)

    def pair_in(kind, i):
        dst, rows = ((wk, 512), (wq, 512), (wv, 512), (wo, 128))[kind]
        ref = dst.at[(y + 1 + i) % ny, pl.ds(pl.multiple_of((1 - core) * rows, rows), rows)]
        return remote(ref, ref, pair_send.at[kind * 3 + i], pair_recv.at[kind * 3 + i], other)

    for ring in narrow + wide:
        ring.begin()

    def hop(way, distance, q, origin):
        ref = held.at[pl.ds(pl.multiple_of(origin * members + q * part, part), part)]
        i = (way * 4 + distance - 1) * nx + q
        return remote(ref, ref, ring_send.at[i], ring_recv.at[i], (up_z, down_z)[way])

    def origin_of(way, distance):
        return (z + nz - distance) % nz if way == 0 else (z + distance) % nz

    def goes(way, distance, q):
        return distance < 4 or (q < nx // 2) == (way == 0)

    for q in range(nx):
        def pre_wait(s, carry):
            @pl.when(s != me)
            def _():
                pre(s, s).wait_recv()
            return carry

        lax.fori_loop(q * part, (q + 1) * part, pre_wait, 0)
        for way in (0, 1):
            hop(way, 1, q, z).start()

    def ring_step(distance):
        for q in range(nx):
            for way in (0, 1):
                if goes(way, distance, q):
                    hop(way, distance, q, origin_of(way, distance)).wait_recv()
                    if distance < 4 and goes(way, distance + 1, q):
                        hop(way, distance + 1, q, origin_of(way, distance)).start()

    for ring in narrow:
        ring.forward()
    ring_step(1)
    for ring in narrow:
        ring.end()
    for ring in across:
        ring.begin()
    for ring in wide:
        ring.forward()
    ring_step(2)
    for ring in across:
        ring.forward()
    ring_step(3)
    for kind, ring in enumerate(wide):
        ring.end()
        for i in range(3):
            pair(kind, i).start()
    ring_step(4)

    rows = pl.ds(pl.multiple_of((me // ny) * 16, 16), 16)
    cols = pl.ds(pl.multiple_of((me % ny) * 256, 256), 256)

    def out(t):
        return remote(outgoing.at[t], listed.at[:, rows, cols], out_send.at[t], out_recv.at[me], member(t))

    def out_in(s):
        there = listed.at[:, pl.ds(pl.multiple_of((s // ny) * 16, 16), 16), pl.ds(pl.multiple_of((s % ny) * 256, 256), 256)]
        return remote(outgoing.at[s], there, out_send.at[s], out_recv.at[s], member(s))

    def pick(t):
        for e in range(LIST_LEN):
            outgoing[t, e] = held[wanted_ref[t * LIST_LEN + e]]

    def out_start(k, carry):
        t = (me + k) % members
        pick(t)
        out(t).start()
        return carry

    lax.fori_loop(1, members, out_start, 0)
    pick(me)
    local = pltpu.make_async_copy(outgoing.at[me], listed.at[:, rows, cols], own_sem.at[4])
    local.start()

    for ring in across:
        ring.end()
    for kind in (2, 3):
        for i in range(3):
            pair(kind, i).start()

    def out_wait(k, carry):
        out_in((me + k) % members).wait_recv()
        return carry

    lax.fori_loop(1, members, out_wait, 0)
    local.wait()
    for kind in range(4):
        for i in range(3):
            pair_in(kind, i).wait_recv()
    for copy in mine:
        copy.wait()

    def drain(k, carry):
        t = (me + k) % members
        pre(t, me).wait_send()
        out(t).wait_send()
        return carry

    lax.fori_loop(1, members, drain, 0)
    for way in (0, 1):
        for distance in range(1, 5):
            for q in range(nx):
                if goes(way, distance, q):
                    hop(way, distance, q, z).wait_send()
    for ring in narrow + wide + across:
        ring.sent()
    for kind in range(4):
        for i in range(3):
            pair(kind, i).wait_send()


def communicate(wanted, tokens, wq, wk, wv, wo):
    members = 32
    vmem = pl.BlockSpec(memory_space=pltpu.VMEM)
    dma = pltpu.SemaphoreType.DMA
    tall = jax.ShapeDtypeStruct((PIX, D, D // PIX), jnp.bfloat16)
    return pl.pallas_call(
        comm_kernel,
        out_shape=(
            jax.ShapeDtypeStruct((LIST_LEN, BLOCK, D), jnp.bfloat16),
            tall, tall, tall,
            jax.ShapeDtypeStruct((PIX, D // PIX, D), jnp.bfloat16),
        ),
        in_specs=[pl.BlockSpec(memory_space=pltpu.SMEM)] + [vmem] * 5,
        out_specs=(vmem,) * 5,
        scratch_shapes=[
            pltpu.VMEM((members, 16, 256), jnp.bfloat16),
            pltpu.VMEM((8 * members, 16, 256), jnp.bfloat16),
            pltpu.VMEM((members, LIST_LEN, 16, 256), jnp.bfloat16),
            dma((members,)), dma((members,)),
            dma((32,)), dma((32,)),
            dma((members,)), dma((members,)),
            dma((24,)), dma((24,)),
            dma((36,)), dma((36,)),
            dma((12,)), dma((12,)),
            dma((5,)),
        ],
        compiler_params=pltpu.CompilerParams(
            collective_id=0, has_side_effects=True, vmem_limit_bytes=40 * 1024 * 1024
        ),
    )(wanted, tokens, wq, wk, wv, wo)


def body(target_tokens, input_tokens, w_query, w_key, w_value, w_out, table, table_block, counts):
    z, y = lax.axis_index("z"), lax.axis_index("pix")
    nx, nz, nc = (lax.axis_size(name) for name in ("x", "z", "core"))
    members = nx * nc * PIX
    place = ((table // 2) % nz) * members + ((table // (2 * nz)) * nc + table % nc) * PIX + table_block
    place = place.reshape(nx, nz, nc * PIX, LIST_LEN)
    wanted = lax.dynamic_index_in_dim(place, z, 1, keepdims=False).reshape(-1)
    listed, wq, wk, wv, wo = communicate(wanted, input_tokens, w_query, w_key, w_value, w_out)
    count = lax.dynamic_slice_in_dim(counts, y, 1, 0)
    return attend(count, target_tokens, listed.reshape(LIST_LEN * BLOCK, D), wq, wk, wv, wo)


def solution(mesh):
    views = ("x", "z", "core")
    fine = Mesh(mesh.devices.reshape(4, 8, 2, 4), ("x", "z", "core", "pix"))
    placed = (
        P((*views, "pix"), None),
        P((*views, "pix"), None),
        P(None, "pix"),
        P(None, "pix"),
        P(None, "pix"),
        P("pix", None),
        P(),
        P(),
        P(views),
    )
    return jax.shard_map(
        body, mesh=fine, in_specs=placed, out_specs=P((*views, "pix"), None), check_vma=False
    )
```

```python
import jax
import jax.numpy as jnp
from jax import lax
from jax.experimental import pallas as pl
from jax.experimental.pallas import tpu as pltpu
from jax.sharding import Mesh, PartitionSpec as P

D = 1024
HEAD_DIM = 64
BLOCK = 128
LIST_LEN = 8
PIX = 4
ROUNDS = 2
ENTRIES = LIST_LEN // ROUNDS


def normalize(tokens):
    source = tokens.astype(jnp.float32)
    center = source - jnp.mean(source, axis=1, keepdims=True)
    spread = jnp.mean(center * center, axis=1, keepdims=True)
    return (center * lax.rsqrt(spread + 1e-05)).astype(jnp.bfloat16)


def kernel(
    table_ref, block_ref, counts_ref, target_ref, tokens_ref, wq_ref, wk_ref, wv_ref, wo_ref,
    result_ref,
    listed, wq, wk, wv, wo, target, tokens, pieces, held, outgoing,
    split, values, scores, probs, total, views, blocks,
    pre_send, pre_recv, ring_send, ring_recv, out_send, out_recv,
    row_send, row_recv, col_send, col_recv, pair_send, pair_recv, own_sem, list_sem,
):
    x, z, core, y = (lax.axis_index(name) for name in ("x", "z", "core", "pix"))
    nx, nz, nc, ny = (lax.axis_size(name) for name in ("x", "z", "core", "pix"))
    members = nx * nc * ny
    me = (x * nc + core) * ny + y
    part = members // nx

    def slab(depth, across):
        return (across * nz + depth) * part

    def member(t):
        return (t // (nc * ny), z, (t // ny) % nc, t % ny)

    up_z, down_z = (x, (z + 1) % nz, core, y), (x, (z + nz - 1) % nz, core, y)
    up_y, down_y = (x, z, core, (y + 1) % ny), (x, z, core, (y + ny - 1) % ny)
    up_x, down_x = ((x + 1) % nx, z, core, y), ((x + nx - 1) % nx, z, core, y)
    other = (x, z, 1 - core, y)

    def remote(src, dst, send, recv, device):
        return pltpu.make_async_remote_copy(
            src_ref=src, dst_ref=dst, send_sem=send, recv_sem=recv,
            device_id=device, device_id_type=pl.DeviceIdType.MESH,
        )

    barrier = pltpu.get_barrier_semaphore()

    def greet(k, carry):
        pl.semaphore_signal(
            barrier, inc=1, device_id=member((me + k) % members), device_id_type=pl.DeviceIdType.MESH
        )
        return carry

    lax.fori_loop(1, members, greet, 0)
    for device in (up_z, down_z):
        pl.semaphore_signal(barrier, inc=1, device_id=device, device_id_type=pl.DeviceIdType.MESH)

    fetch = pltpu.make_async_copy(tokens_ref, tokens, own_sem.at[6])
    fetch.start()
    lists = [
        pltpu.make_async_copy(
            src, dst, list_sem.at[kind]
        )
        for kind, (src, dst) in enumerate(((table_ref, views), (block_ref, blocks)))
    ]
    mine = [
        pltpu.make_async_copy(src, dst.at[y], own_sem.at[i])
        for i, (src, dst) in enumerate(((wq_ref, wq), (wk_ref, wk), (wv_ref, wv), (wo_ref, wo)))
    ]
    mine.append(pltpu.make_async_copy(target_ref, target, own_sem.at[4]))
    for copy in lists + mine:
        copy.start()
    fetch.wait()
    normed = normalize(tokens[...])
    for row in range(members // ny):
        for col in range(ny):
            pieces[row * ny + col] = normed[row * 16:(row + 1) * 16, col * 256:(col + 1) * 256]
    held[slab(z, x) + core * ny + y] = pieces[me]
    pl.semaphore_wait(barrier, members - 1 + 2)

    def pre(t, s):
        return remote(pieces.at[t], held.at[slab(z, s // part) + s % part], pre_send.at[t], pre_recv.at[s], member(t))

    def pre_start(k, carry):
        pre((me + k) % members, me).start()
        return carry

    lax.fori_loop(1, members, pre_start, 0)

    class Ring:
        def __init__(self, own, slot, at, up, down, send, recv, base):
            self.own, self.slot, self.at, self.up, self.down = own, slot, at, up, down
            self.send, self.recv, self.base = send, recv, base

        def copy(self, i, origin, half, device, src=None):
            dst = self.slot(origin, half)
            return remote(
                dst if src is None else src, dst, self.send.at[self.base + i], self.recv.at[self.base + i], device
            )

        def begin(self):
            for half in (0, 1):
                self.copy(half, self.at, half, self.up, self.own(half)).start()
                self.copy(3 + half, self.at, half, self.down, self.own(half)).start()

        def forward(self):
            before, after = (self.at + 3) % 4, (self.at + 1) % 4
            self.copy(0, before, 0, self.up).wait_recv()
            self.copy(2, before, 0, self.up).start()
            self.copy(4, after, 1, self.down).wait_recv()
            self.copy(5, after, 1, self.down).start()

        def end(self):
            before, after, far = (self.at + 3) % 4, (self.at + 1) % 4, (self.at + 2) % 4
            self.copy(1, before, 1, self.up).wait_recv()
            self.copy(3, after, 0, self.down).wait_recv()
            self.copy(2, far, 0, self.up).wait_recv()
            self.copy(5, far, 1, self.down).wait_recv()

        def sent(self):
            for i in range(6):
                self.copy(i, self.at, i % 2, self.up).wait_send()

    def y_ring(src, dst, start, size, base):
        return Ring(
            lambda half: src.at[pl.ds(start + half * size, size)],
            lambda origin, half: dst.at[origin, pl.ds(start + half * size, size)],
            y, up_y, down_y, row_send, row_recv, base,
        )

    def x_ring(dst, quarter, first, size, base):
        def slot(origin, half):
            return dst.at[quarter, pl.ds(pl.multiple_of(first + origin * 2 * size + half * size, size), size)]

        return Ring(lambda half: slot(x, half), slot, x, up_x, down_x, col_send, col_recv, base)

    narrow = [
        y_ring(wv_ref, wv, pl.multiple_of(core * 512 + x * 128, 128), 64, 0),
        y_ring(wo_ref, wo, pl.multiple_of(core * 128 + x * 32, 32), 16, 6),
    ]
    wide = [
        y_ring(wk_ref, wk, pl.multiple_of(core * 512, 512), 256, 12),
        y_ring(wq_ref, wq, pl.multiple_of(core * 512, 512), 256, 18),
    ]
    across = [
        x_ring(dst, (y + 1 + i) % ny, pl.multiple_of(core * 8 * size, 8 * size), size, (3 * kind + i) * 6)
        for kind, (dst, size) in enumerate(((wv, 64), (wo, 16)))
        for i in range(3)
    ]

    def pair(kind, i):
        dst, rows = ((wk, 512), (wq, 512), (wv, 512), (wo, 128))[kind]
        ref = dst.at[(y + 1 + i) % ny, pl.ds(pl.multiple_of(core * rows, rows), rows)]
        return remote(ref, ref, pair_send.at[kind * 3 + i], pair_recv.at[kind * 3 + i], other)

    def pair_in(kind, i):
        dst, rows = ((wk, 512), (wq, 512), (wv, 512), (wo, 128))[kind]
        ref = dst.at[(y + 1 + i) % ny, pl.ds(pl.multiple_of((1 - core) * rows, rows), rows)]
        return remote(ref, ref, pair_send.at[kind * 3 + i], pair_recv.at[kind * 3 + i], other)

    for ring in narrow + wide:
        ring.begin()

    def turn(q):
        return (x + nx - q) % nx

    def hop(way, distance, q, origin):
        ref = held.at[pl.ds(pl.multiple_of(slab(origin, turn(q)), part), part)]
        i = (way * 4 + distance - 1) * nx + q
        return remote(ref, ref, ring_send.at[i], ring_recv.at[i], (up_z, down_z)[way])

    def origin_of(way, distance):
        return (z + nz - distance) % nz if way == 0 else (z + distance) % nz

    def goes(way, distance, q):
        return distance < 4 or (q < nx // 2) == (way == 0)

    for q in range(nx):
        def pre_wait(s, carry):
            @pl.when(s != me)
            def _():
                pre(s, s).wait_recv()
            return carry

        first = turn(q) * part
        lax.fori_loop(first, first + part, pre_wait, 0)
        for way in (0, 1):
            hop(way, 1, q, z).start()

    def ring_step(distance):
        for q in range(nx):
            for way in (0, 1):
                if goes(way, distance, q):
                    hop(way, distance, q, origin_of(way, distance)).wait_recv()
                    if distance < 4 and goes(way, distance + 1, q):
                        hop(way, distance + 1, q, origin_of(way, distance)).start()

    for ring in narrow:
        ring.forward()
    ring_step(1)
    for ring in narrow:
        ring.end()
    for ring in across:
        ring.begin()
    for ring in wide:
        ring.forward()
    ring_step(2)
    for ring in across:
        ring.forward()
    ring_step(3)
    for kind, ring in enumerate(wide):
        ring.end()
        for i in range(3):
            pair(kind, i).start()
    ring_step(4)

    for copy in lists:
        copy.wait()

    def spot(r, s):
        return listed.at[
            pl.ds(r * ENTRIES, ENTRIES),
            pl.ds(pl.multiple_of((s // ny) * 16, 16), 16),
            pl.ds(pl.multiple_of((s % ny) * 256, 256), 256),
        ]

    def out(r, t, s):
        i = r * members
        return remote(outgoing.at[r, t], spot(r, s), out_send.at[i + t], out_recv.at[i + s], member(t))

    def pick(r, t):
        row = slab(z, t // part) + t % part
        for e in range(ENTRIES):
            entry = r * ENTRIES + e
            outgoing[r, t, e] = held[views[entry, row] * ny + blocks[entry, row]]

    local = []
    for r in range(ROUNDS):

        def out_start(k, carry):
            t = (me + k) % members
            pick(r, t)
            out(r, t, me).start()
            return carry

        lax.fori_loop(1, members, out_start, 0)
        pick(r, me)
        local.append(pltpu.make_async_copy(outgoing.at[r, me], spot(r, me), own_sem.at[7 + r]))
        local[r].start()

    for ring in across:
        ring.end()
    for kind in (2, 3):
        for i in range(3):
            pair(kind, i).start()

    for copy in mine:
        copy.wait()
    for kind in (1, 0, 2):
        for i in range(3):
            pair_in(kind, i).wait_recv()

    aim = normalize(target[...])
    wide_cols = D // PIX
    group_heads = wide_cols // HEAD_DIM
    lane_head = lax.broadcasted_iota(jnp.int32, (1, wide_cols), 1) // HEAD_DIM
    for g in range(PIX):
        query = jnp.dot(aim, wq[g], preferred_element_type=jnp.float32)
        for h in range(group_heads):
            split[g, h * BLOCK:(h + 1) * BLOCK] = jnp.where(lane_head == h, query, 0.0).astype(jnp.bfloat16)

    span = ENTRIES * BLOCK
    for r in range(ROUNDS):

        def out_wait(k, carry):
            s = (me + k) % members
            out(r, s, s).wait_recv()
            return carry

        lax.fori_loop(1, members, out_wait, 0)
        local[r].wait()
        rows = listed[r * ENTRIES:(r + 1) * ENTRIES].reshape(span, D)
        at = slice(r * span, (r + 1) * span)
        for g in range(PIX):
            key = jnp.dot(rows, wk[g], preferred_element_type=jnp.float32).astype(jnp.bfloat16)
            values[g, at] = jnp.dot(rows, wv[g], preferred_element_type=jnp.float32).astype(jnp.bfloat16)
            scores[g, :, at] = lax.dot_general(
                split[g], key, (((1,), (1,)), ((), ())), preferred_element_type=jnp.float32
            )

    columns = lax.broadcasted_iota(jnp.int32, (1, LIST_LEN * BLOCK), 1)
    shade = jnp.where(columns < counts_ref[y] * BLOCK, 0.0, -1e30)
    chunk = 32

    def soften(i, carry):
        g, at = i // (group_heads * BLOCK // chunk), i % (group_heads * BLOCK // chunk)
        rows = pl.ds(pl.multiple_of(at * chunk, chunk), chunk)
        logits = scores[g, rows] * HEAD_DIM ** (-0.5) + shade
        weights = jnp.exp(logits - jnp.max(logits, axis=1, keepdims=True))
        probs[g, rows] = (weights * (1.0 / jnp.sum(weights, axis=1, keepdims=True))).astype(jnp.bfloat16)
        return carry

    lax.fori_loop(0, PIX * group_heads * BLOCK // chunk, soften, 0)
    for i in range(3):
        pair_in(3, i).wait_recv()
    mixed = jnp.zeros((BLOCK, D), jnp.float32)
    for g in range(PIX):
        summed = jnp.dot(probs[g], values[g], preferred_element_type=jnp.float32)
        attended = jnp.zeros((BLOCK, wide_cols), jnp.float32)
        for h in range(group_heads):
            attended = jnp.where(lane_head == h, summed[h * BLOCK:(h + 1) * BLOCK], attended)
        mixed += jnp.dot(attended.astype(jnp.bfloat16), wo[g], preferred_element_type=jnp.float32)
    total[...] = (target[...].astype(jnp.float32) + mixed).astype(jnp.bfloat16)
    deliver = pltpu.make_async_copy(total, result_ref, own_sem.at[5])
    deliver.start()

    def drain(k, carry):
        t = (me + k) % members
        pre(t, me).wait_send()
        for r in range(ROUNDS):
            out(r, t, me).wait_send()
        return carry

    lax.fori_loop(1, members, drain, 0)
    for way in (0, 1):
        for distance in range(1, 5):
            for q in range(nx):
                if goes(way, distance, q):
                    hop(way, distance, q, z).wait_send()
    for ring in narrow + wide + across:
        ring.sent()
    for kind in range(4):
        for i in range(3):
            pair(kind, i).wait_send()
    deliver.wait()


def body(target_tokens, input_tokens, w_query, w_key, w_value, w_out, table, table_block, counts):
    members = 32
    cols = D // PIX
    smem, hbm = pl.BlockSpec(memory_space=pltpu.SMEM), pl.BlockSpec(memory_space=pltpu.HBM)
    dma = pltpu.SemaphoreType.DMA
    tall = pltpu.VMEM((PIX, D, cols), jnp.bfloat16)
    block = pltpu.VMEM((BLOCK, D), jnp.bfloat16)
    listed_rows = LIST_LEN * BLOCK
    return pl.pallas_call(
        kernel,
        out_shape=jax.ShapeDtypeStruct((BLOCK, D), jnp.bfloat16),
        in_specs=[hbm, hbm, smem] + [hbm] * 6,
        out_specs=hbm,
        scratch_shapes=[
            pltpu.VMEM((LIST_LEN, BLOCK, D), jnp.bfloat16),
            tall, tall, tall,
            pltpu.VMEM((PIX, cols, D), jnp.bfloat16),
            block, block,
            pltpu.VMEM((members, 16, cols), jnp.bfloat16),
            pltpu.VMEM((8 * members, 16, cols), jnp.bfloat16),
            pltpu.VMEM((ROUNDS, members, ENTRIES, 16, cols), jnp.bfloat16),
            pltpu.VMEM((PIX, 4 * BLOCK, cols), jnp.bfloat16),
            pltpu.VMEM((PIX, listed_rows, cols), jnp.bfloat16),
            pltpu.VMEM((PIX, 4 * BLOCK, listed_rows), jnp.float32),
            pltpu.VMEM((PIX, 4 * BLOCK, listed_rows), jnp.bfloat16),
            block,
            pltpu.SMEM((LIST_LEN, 8 * members), jnp.int32),
            pltpu.SMEM((LIST_LEN, 8 * members), jnp.int32),
            dma((members,)), dma((members,)),
            dma((32,)), dma((32,)),
            dma((ROUNDS * members,)), dma((ROUNDS * members,)),
            dma((24,)), dma((24,)),
            dma((36,)), dma((36,)),
            dma((12,)), dma((12,)),
            dma((7 + ROUNDS,)), dma((2,)),
        ],
        compiler_params=pltpu.CompilerParams(
            collective_id=0, has_side_effects=True, vmem_limit_bytes=60 * 1024 * 1024
        ),
        cost_estimate=pl.CostEstimate(flops=5_400_000_000, bytes_accessed=3 << 20, transcendentals=2 << 20),
    )(table.T, table_block.T, counts, target_tokens, input_tokens, w_query, w_key, w_value, w_out)


def solution(mesh):
    views = ("x", "z", "core")
    fine = Mesh(mesh.devices.reshape(4, 8, 2, 4), ("x", "z", "core", "pix"))
    placed = (
        P((*views, "pix"), None),
        P((*views, "pix"), None),
        P(None, "pix"),
        P(None, "pix"),
        P(None, "pix"),
        P("pix", None),
        P(),
        P(),
        P(views),
    )
    return jax.shard_map(
        body, mesh=fine, in_specs=placed, out_specs=P((*views, "pix"), None), check_vma=False
    )
```

```python
import jax
import jax.numpy as jnp
from jax import lax
from jax.experimental import pallas as pl
from jax.experimental.pallas import tpu as pltpu
from jax.sharding import Mesh, PartitionSpec as P

D = 1024
HEAD_DIM = 64
BLOCK = 128
LIST_LEN = 8
PIX = 4
HALVES = 2
STRIDE = 11
HALF_ROWS = BLOCK // HALVES
CHUNK = 256
LOG2E = 1.4426950408889634


def normalize(tokens):
    source = tokens.astype(jnp.float32)
    center = source - jnp.mean(source, axis=1, keepdims=True)
    spread = jnp.mean(center * center, axis=1, keepdims=True)
    return (center * lax.rsqrt(spread + 1e-05)).astype(jnp.bfloat16)


def kernel(
    table_ref, block_ref, counts_ref, target_ref, tokens_ref, wq_ref, wk_ref, wv_ref, wo_ref,
    result_ref,
    listed, wq, wk, wv, wo, target, tokens, pieces, held, outgoing,
    split, values, scores, probs, peaks, sums, total, views, blocks,
    pre_send, pre_recv, ring_send, ring_recv, out_send, out_recv,
    row_send, row_recv, col_send, col_recv, far_send, far_recv, pair_send, pair_recv, own_sem,
):
    x, z, core, y = (lax.axis_index(name) for name in ("x", "z", "core", "pix"))
    nx, nz, nc, ny = (lax.axis_size(name) for name in ("x", "z", "core", "pix"))
    part = nc * ny
    members = nx * part
    me = x * part + core * ny + y

    def member(t):
        return (t // part, z, (t // ny) % nc, t % ny)

    up_z, down_z = (x, (z + 1) % nz, core, y), (x, (z + nz - 1) % nz, core, y)
    up_y, down_y = (x, z, core, (y + 1) % ny), (x, z, core, (y + ny - 1) % ny)
    up_x, down_x = ((x + 1) % nx, z, core, y), ((x + nx - 1) % nx, z, core, y)
    other = (x, z, 1 - core, y)

    def remote(src, dst, send, recv, device):
        return pltpu.make_async_remote_copy(
            src_ref=src, dst_ref=dst, send_sem=send, recv_sem=recv,
            device_id=device, device_id_type=pl.DeviceIdType.MESH,
        )

    fetch = pltpu.make_async_copy(tokens_ref, tokens, own_sem.at[0])
    fetch.start()
    barrier = pltpu.get_barrier_semaphore()

    def greet(k, carry):
        pl.semaphore_signal(
            barrier, inc=1, device_id=member((me + k) % members), device_id_type=pl.DeviceIdType.MESH
        )
        return carry

    lax.fori_loop(1, members, greet, 0)
    for device in (up_z, down_z):
        pl.semaphore_signal(barrier, inc=1, device_id=device, device_id_type=pl.DeviceIdType.MESH)

    lists = [
        pltpu.make_async_copy(src, dst, own_sem.at[1 + i])
        for i, (src, dst) in enumerate(((table_ref, views), (block_ref, blocks)))
    ]
    mine = [
        pltpu.make_async_copy(src, dst, own_sem.at[3 + i])
        for i, (src, dst) in enumerate(
            ((wq_ref, wq.at[ny - 1]), (wk_ref, wk.at[ny - 1]), (wv_ref, wv.at[ny - 1]), (wo_ref, wo.at[ny - 1]), (target_ref, target))
        )
    ]
    for copy in lists + mine:
        copy.start()
    fetch.wait()
    normed = normalize(tokens[...])
    for t in range(members):
        for half in range(HALVES):
            top, left = half * HALF_ROWS + (t // part) * 16, (t % part) * 128
            pieces[t, half] = normed[top:top + 16, left:left + 128]
    held[x, z * part + core * ny + y] = pieces[me]
    pl.semaphore_wait(barrier, members - 1 + 2)

    def pre(t, s):
        return remote(
            pieces.at[t], held.at[s // part, z * part + s % part], pre_send.at[t], pre_recv.at[s], member(t)
        )

    def pre_start(k, carry):
        pre((me + k) % members, me).start()
        return carry

    lax.fori_loop(1, members, pre_start, 0)

    class Ring:
        def __init__(self, own, slot, at, up, down, send, recv, base):
            self.own, self.slot, self.at, self.up, self.down = own, slot, at, up, down
            self.send, self.recv, self.base = send, recv, base

        def copy(self, i, src, origin, rel, half, device):
            dst = self.slot(origin % 4, rel, half)
            return remote(
                dst if src is None else src, dst, self.send.at[self.base + i], self.recv.at[self.base + i], device
            )

        def begin(self):
            for half in (0, 1):
                self.copy(half, self.own(half), self.at, 3, half, self.up).start()
                self.copy(3 + half, self.own(half), self.at, 1, half, self.down).start()

        def forward(self):
            before, after = (self.at + 3) % 4, (self.at + 1) % 4
            self.copy(0, None, before, 3, 0, self.up).wait_recv()
            self.copy(2, self.slot(before, 3, 0), before, 2, 0, self.up).start()
            self.copy(4, None, after, 1, 1, self.down).wait_recv()
            self.copy(5, self.slot(after, 1, 1), after, 2, 1, self.down).start()

        def end(self):
            self.copy(1, None, self.at + 3, 3, 1, self.up).wait_recv()
            self.copy(3, None, self.at + 1, 1, 0, self.down).wait_recv()
            self.copy(2, None, self.at + 2, 2, 0, self.up).wait_recv()
            self.copy(5, None, self.at + 2, 2, 1, self.down).wait_recv()

        def sent(self):
            for i in range(6):
                self.copy(i, None, self.at + 2, 2, (0, 1, 0, 0, 1, 1)[i], self.up).wait_send()

    def y_ring(src, dst, start, size, base):
        return Ring(
            lambda half: src.at[pl.ds(start + half * size, size)],
            lambda origin, rel, half: dst.at[rel - 1, pl.ds(start + half * size, size)],
            y, up_y, down_y, row_send, row_recv, base,
        )

    def x_ring(dst, base):
        def slot(origin, rel, half):
            return dst.at[pl.ds(0, 3), pl.ds(pl.multiple_of(core * 512 + origin * 128 + half * 64, 64), 64)]

        return Ring(lambda half: slot(x, 0, half), slot, x, up_x, down_x, col_send, col_recv, base)

    sixteenth = pl.ds(pl.multiple_of(core * 128 + z * 16, 16), 16)
    narrow = [y_ring(src, dst, pl.multiple_of(core * 512 + x * 128, 128), 64, 6 * i)
              for i, (src, dst) in enumerate(((wq_ref, wq), (wv_ref, wv)))]
    wide = y_ring(wk_ref, wk, pl.multiple_of(core * 512, 512), 256, 12)
    thin = Ring(
        lambda half: wo_ref.at[sixteenth, pl.ds(half * 512, 512)],
        lambda origin, rel, half: wo.at[rel - 1, sixteenth, pl.ds(half * 512, 512)],
        y, up_y, down_y, row_send, row_recv, 18,
    )
    across = [x_ring(dst, 6 * i) for i, dst in enumerate((wq, wv))]

    def pair(kind, side):
        dst, rows = ((wq, 512), (wk, 512), (wv, 512), (wo, 128))[kind]
        ref = dst.at[pl.ds(0, 3), pl.ds(pl.multiple_of(side * rows, rows), rows)]
        return remote(ref, ref, pair_send.at[kind], pair_recv.at[kind], other)

    for ring in (*narrow, wide, thin):
        ring.begin()

    def turn(q):
        return (x + nx - q) % nx

    def hop(way, distance, q, origin):
        ref = held.at[turn(q), pl.ds(pl.multiple_of(origin * part, part), part)]
        i = (way * 4 + distance - 1) * nx + q
        return remote(ref, ref, ring_send.at[i], ring_recv.at[i], (up_z, down_z)[way])

    def origin_of(way, distance):
        return (z + nz - distance) % nz if way == 0 else (z + distance) % nz

    def goes(way, distance, q):
        return distance < 4 or (q < nx // 2) == (way == 0)

    def ring_begin(q):
        for way in (0, 1):
            hop(way, 1, q, z).start()

    def ring_step(distance):
        for q in range(nx):
            for way in (0, 1):
                if goes(way, distance, q):
                    hop(way, distance, q, origin_of(way, distance)).wait_recv()
                    if distance < 4 and goes(way, distance + 1, q):
                        hop(way, distance + 1, q, origin_of(way, distance)).start()

    def wo_hop(way, distance, origin):
        rows = pl.ds(pl.multiple_of(core * 128 + origin * 16, 16), 16)
        cols = pl.ds(0, D) if distance < 4 else pl.ds(way * 512, 512)
        ref = wo.at[pl.ds(0, 3), rows, cols]
        i = way * 4 + distance - 1
        return remote(ref, ref, far_send.at[i], far_recv.at[i], (up_z, down_z)[way])

    def wo_step(distance):
        for way in (0, 1):
            origin = origin_of(way, distance)
            if distance > 0:
                wo_hop(way, distance, origin).wait_recv()
            if distance < 4:
                wo_hop(way, distance + 1, origin).start()

    def spot(half, s):
        return listed.at[
            half, :,
            pl.ds(pl.multiple_of((s // part) * 16, 16), 16),
            pl.ds(pl.multiple_of((s % part) * 128, 128), 128),
        ]

    def out(half, t, s):
        i = half * members
        return remote(outgoing.at[half, t], spot(half, s), out_send.at[i + t], out_recv.at[i + s], member(t))

    def pick(half, t):
        row = (t // part * nz + z) * part + t % part
        for e in range(LIST_LEN):
            view = views[e, row]
            outgoing[half, t, e] = held[view // 16, view % 16 * ny + blocks[e, row], half]

    def deal(half):
        def start(k, carry):
            t = (me + k * STRIDE) % members
            pick(half, t)
            out(half, t, me).start()
            return carry

        lax.fori_loop(1, members, start, 0)
        pick(half, me)
        copy = pltpu.make_async_copy(outgoing.at[half, me], spot(half, me), own_sem.at[9 + half])
        copy.start()
        return copy

    for q in range(nx):
        def pre_wait(s, carry):
            @pl.when(s != me)
            def _():
                pre(s, s).wait_recv()
            return carry

        first = turn(q) * part
        lax.fori_loop(first, first + part, pre_wait, 0)
        ring_begin(q)

    ring_step(1)
    for ring in narrow:
        ring.forward()
    ring_step(2)
    for ring, far in zip(narrow, across):
        ring.end()
        far.begin()
    wide.forward()
    thin.forward()
    ring_step(3)
    for ring in across:
        ring.forward()
    for copy in lists:
        copy.wait()
    ring_step(4)
    local = [deal(0)]
    thin.end()
    wo_step(0)
    local.append(deal(1))
    wide.end()
    pair(1, core).start()
    for kind, ring in ((2, across[1]), (0, across[0])):
        ring.end()
        pair(kind, core).start()
    wo_step(1)

    for copy in mine:
        copy.wait()
    pair(0, 1 - core).wait_recv()
    wide_cols = D // ny
    group_heads = wide_cols // HEAD_DIM
    lane_head = lax.broadcasted_iota(jnp.int32, (1, wide_cols), 1) // HEAD_DIM
    aim = normalize(target[...])
    for g in range(ny):
        query = jnp.dot(aim, wq[g], preferred_element_type=jnp.float32)
        for h in range(group_heads):
            split[g, h * BLOCK:(h + 1) * BLOCK] = jnp.where(lane_head == h, query, 0.0).astype(jnp.bfloat16)
    wo_step(2)
    for kind in (1, 2):
        pair(kind, 1 - core).wait_recv()

    span = LIST_LEN * HALF_ROWS
    columns = lax.broadcasted_iota(jnp.int32, (1, span), 1)
    shade = jnp.where(columns < counts_ref[y] * HALF_ROWS, 0.0, -1e30)
    stretch = HEAD_DIM ** (-0.5) * LOG2E

    def arrive(half):
        def wait(k, carry):
            s = (me + k) % members
            out(half, s, s).wait_recv()
            return carry

        lax.fori_loop(1, members, wait, 0)
        local[half].wait()

    def project(half):
        rows = listed[half].reshape(span, D)
        at = slice(half * span, (half + 1) * span)
        for g in range(ny):
            key = jnp.dot(rows, wk[g], preferred_element_type=jnp.float32).astype(jnp.bfloat16)
            values[g, at] = jnp.dot(rows, wv[g], preferred_element_type=jnp.float32).astype(jnp.bfloat16)
            scores[g, :, at] = lax.dot_general(
                split[g], key, (((1,), (1,)), ((), ())), preferred_element_type=jnp.float32
            )

    per_group = group_heads * BLOCK // CHUNK

    def chunk_at(i):
        return i // per_group, pl.ds(pl.multiple_of(i % per_group * CHUNK, CHUNK), CHUNK)

    def soften(i, carry):
        g, rows = chunk_at(i)
        logits = scores[g, rows, 0:span] + shade
        peak = jnp.max(logits, axis=1, keepdims=True)
        weights = jnp.exp2((logits - peak) * stretch)
        scores[g, rows, 0:span] = weights
        peaks[g, rows] = jnp.broadcast_to(peak, (CHUNK, 128))
        sums[g, rows] = jnp.broadcast_to(jnp.sum(weights, axis=1, keepdims=True), (CHUNK, 128))
        return carry

    def finish(g, rows):
        logits = scores[g, rows, span:2 * span] + shade
        before = peaks[g, rows][:, 0:1]
        peak = jnp.maximum(before, jnp.max(logits, axis=1, keepdims=True))
        weights = jnp.exp2((logits - peak) * stretch)
        fade = jnp.exp2((before - peak) * stretch)
        whole = fade * sums[g, rows][:, 0:1] + jnp.sum(weights, axis=1, keepdims=True)
        share = 1.0 / whole
        probs[g, rows, span:2 * span] = (weights * share).astype(jnp.bfloat16)
        probs[g, rows, 0:span] = (scores[g, rows, 0:span] * (fade * share)).astype(jnp.bfloat16)

    arrive(0)
    project(0)
    wo_step(3)
    lax.fori_loop(0, ny * per_group, soften, 0)
    wo_step(4)
    pair(3, core).start()
    arrive(1)
    project(1)
    pair(3, 1 - core).wait_recv()
    mixed = jnp.zeros((BLOCK, D), jnp.float32)
    for g in range(ny):
        for h in range(group_heads):
            finish(g, slice(h * BLOCK, (h + 1) * BLOCK))
        summed = jnp.dot(probs[g], values[g], preferred_element_type=jnp.float32)
        attended = jnp.zeros((BLOCK, wide_cols), jnp.float32)
        for h in range(group_heads):
            attended = jnp.where(lane_head == h, summed[h * BLOCK:(h + 1) * BLOCK], attended)
        mixed += jnp.dot(attended.astype(jnp.bfloat16), wo[g], preferred_element_type=jnp.float32)
    total[...] = (target[...].astype(jnp.float32) + mixed).astype(jnp.bfloat16)
    deliver = pltpu.make_async_copy(total, result_ref, own_sem.at[8])
    deliver.start()

    def drain(k, carry):
        t = (me + k) % members
        pre(t, me).wait_send()
        for half in range(HALVES):
            out(half, t, me).wait_send()
        return carry

    lax.fori_loop(1, members, drain, 0)
    for way in (0, 1):
        for distance in range(1, 5):
            for q in range(nx):
                if goes(way, distance, q):
                    hop(way, distance, q, z).wait_send()
    for way in (0, 1):
        for distance in range(1, 5):
            wo_hop(way, distance, z).wait_send()
    for ring in (*narrow, wide, thin, *across):
        ring.sent()
    for kind in range(4):
        pair(kind, core).wait_send()
    deliver.wait()


def body(target_tokens, input_tokens, w_query, w_key, w_value, w_out, table, table_block, counts):
    members = 32
    cols = D // PIX
    smem, hbm = pl.BlockSpec(memory_space=pltpu.SMEM), pl.BlockSpec(memory_space=pltpu.HBM)
    dma = pltpu.SemaphoreType.DMA
    tall = pltpu.VMEM((PIX, D, cols), jnp.bfloat16)
    block = pltpu.VMEM((BLOCK, D), jnp.bfloat16)
    listed_rows = LIST_LEN * BLOCK
    stats = pltpu.VMEM((PIX, 4 * BLOCK, 128), jnp.float32)
    return pl.pallas_call(
        kernel,
        out_shape=jax.ShapeDtypeStruct((BLOCK, D), jnp.bfloat16),
        in_specs=[hbm, hbm, smem] + [hbm] * 6,
        out_specs=hbm,
        scratch_shapes=[
            pltpu.VMEM((HALVES, LIST_LEN, HALF_ROWS, D), jnp.bfloat16),
            tall, tall, tall,
            pltpu.VMEM((PIX, cols, D), jnp.bfloat16),
            block, block,
            pltpu.VMEM((members, HALVES, 16, 128), jnp.bfloat16),
            pltpu.VMEM((4, 64, HALVES, 16, 128), jnp.bfloat16),
            pltpu.VMEM((HALVES, members, LIST_LEN, 16, 128), jnp.bfloat16),
            pltpu.VMEM((PIX, 4 * BLOCK, cols), jnp.bfloat16),
            pltpu.VMEM((PIX, listed_rows, cols), jnp.bfloat16),
            pltpu.VMEM((PIX, 4 * BLOCK, listed_rows), jnp.float32),
            pltpu.VMEM((PIX, 4 * BLOCK, listed_rows), jnp.bfloat16),
            stats, stats,
            block,
            pltpu.SMEM((LIST_LEN, 8 * members), jnp.int32),
            pltpu.SMEM((LIST_LEN, 8 * members), jnp.int32),
            dma((members,)), dma((members,)),
            dma((32,)), dma((32,)),
            dma((HALVES * members,)), dma((HALVES * members,)),
            dma((24,)), dma((24,)),
            dma((12,)), dma((12,)),
            dma((8,)), dma((8,)),
            dma((4,)), dma((4,)),
            dma((9 + HALVES,)),
        ],
        compiler_params=pltpu.CompilerParams(
            collective_id=0, has_side_effects=True, vmem_limit_bytes=60 * 1024 * 1024
        ),
        cost_estimate=pl.CostEstimate(flops=5_400_000_000, bytes_accessed=3 << 20, transcendentals=2 << 20),
    )(table.T, table_block.T, counts, target_tokens, input_tokens, w_query, w_key, w_value, w_out)


def solution(mesh):
    views = ("x", "z", "core")
    fine = Mesh(mesh.devices.reshape(4, 8, 2, 4), ("x", "z", "core", "pix"))
    placed = (
        P((*views, "pix"), None),
        P((*views, "pix"), None),
        P(None, "pix"),
        P(None, "pix"),
        P(None, "pix"),
        P("pix", None),
        P(),
        P(),
        P(views),
    )
    return jax.shard_map(
        body, mesh=fine, in_specs=placed, out_specs=P((*views, "pix"), None), check_vma=False
    )
```

```python
import jax
import jax.numpy as jnp
from jax import lax
from jax.experimental import pallas as pl
from jax.experimental.pallas import tpu as pltpu
from jax.sharding import Mesh, PartitionSpec as P

D = 1024
HEAD_DIM = 64
BLOCK = 128
LIST_LEN = 8
PIX = 4
HALVES = 2
STRIDE = 11
HALF_ROWS = BLOCK // HALVES
CHUNK = 256
LOG2E = 1.4426950408889634


def normalize(tokens):
    source = tokens.astype(jnp.float32)
    center = source - jnp.mean(source, axis=1, keepdims=True)
    spread = jnp.mean(center * center, axis=1, keepdims=True)
    return (center * lax.rsqrt(spread + 1e-05)).astype(jnp.bfloat16)


def mod(value, power):
    return value % power if isinstance(value, int) else value & (power - 1)


def over(value, power):
    return value // power if isinstance(value, int) else value >> (power.bit_length() - 1)


def kernel(
    table_ref, block_ref, counts_ref, target_ref, tokens_ref, wq_ref, wk_ref, wv_ref, wo_ref,
    result_ref,
    listed, wq, wk, wv, wo, target, tokens, pieces, held, held_b, outgoing,
    split, values, scores, probs, peaks, sums, total, views, blocks,
    pre_send, pre_recv, ring_send, ring_recv, out_send, out_recv,
    row_send, row_recv, col_send, col_recv, slab_send, slab_recv, pair_send, pair_recv, own_sem,
):
    x, z, core, y = (lax.axis_index(name) for name in ("x", "z", "core", "pix"))
    nx, nz, nc, ny = (lax.axis_size(name) for name in ("x", "z", "core", "pix"))
    part = nc * ny
    members = nx * part
    places = (x * part + core * ny + y, z * ny + y)

    def member(half, t):
        if half == 0:
            return (over(t, part), z, mod(over(t, ny), nc), mod(t, ny))
        return (x, over(t, ny), core, mod(t, ny))

    up_z, down_z = (x, mod(z + 1, nz), core, y), (x, mod(z + nz - 1, nz), core, y)
    up_y, down_y = (x, z, core, mod(y + 1, ny)), (x, z, core, mod(y + ny - 1, ny))
    up_x, down_x = (mod(x + 1, nx), z, core, y), (mod(x + nx - 1, nx), z, core, y)
    other = (x, z, 1 - core, y)

    def remote(src, dst, send, recv, device):
        return pltpu.make_async_remote_copy(
            src_ref=src, dst_ref=dst, send_sem=send, recv_sem=recv,
            device_id=device, device_id_type=pl.DeviceIdType.MESH,
        )

    fetch = pltpu.make_async_copy(tokens_ref, tokens, own_sem.at[0])
    fetch.start()
    barrier = pltpu.get_barrier_semaphore()

    def greet(k, carry):
        for half in range(HALVES):
            pl.semaphore_signal(
                barrier, inc=1, device_id=member(half, mod(places[half] + k, members)),
                device_id_type=pl.DeviceIdType.MESH,
            )
        return carry

    for k in range(1, members):
        greet(k, 0)
    lists = [
        pltpu.make_async_copy(src, dst, own_sem.at[1 + i])
        for i, (src, dst) in enumerate(((table_ref, views), (block_ref, blocks)))
    ]
    mine = [
        pltpu.make_async_copy(src, dst, own_sem.at[3 + i])
        for i, (src, dst) in enumerate(
            ((wq_ref, wq.at[ny - 1]), (wk_ref, wk.at[ny - 1]), (wv_ref, wv.at[ny - 1]), (wo_ref, wo.at[ny - 1]), (target_ref, target))
        )
    ]
    for copy in lists + mine:
        copy.start()
    fetch.wait()
    normed = normalize(tokens[...])
    for t in range(members):
        for half in range(HALVES):
            top, left = half * HALF_ROWS + (over(t, part)) * 16, (mod(t, part)) * 128
            pieces[t, half] = normed[top:top + 16, left:left + 128]
    held[x, z * part + core * ny + y] = pieces[places[0], 0]
    held_b[x * nc + core, places[1]] = pieces[places[1], 1]
    pl.semaphore_wait(barrier, HALVES * (members - 1))

    def pre(half, t, s):
        dst = held.at[over(s, part), z * part + mod(s, part)] if half == 0 else held_b.at[x * nc + core, s]
        i = half * members
        return remote(pieces.at[t, half], dst, pre_send.at[i + t], pre_recv.at[i + s], member(half, t))

    def pre_start(k, carry):
        for half in (1, 0):
            pre(half, mod(places[half] + k, members), places[half]).start()
        return carry

    for k in range(1, members):
        pre_start(k, 0)

    class Ring:
        def __init__(self, own, slot, at, up, down, send, recv, base):
            self.own, self.slot, self.at, self.up, self.down = own, slot, at, up, down
            self.send, self.recv, self.base = send, recv, base

        def copy(self, i, src, origin, rel, half, device):
            dst = self.slot(mod(origin, 4), rel, half)
            return remote(
                dst if src is None else src, dst, self.send.at[self.base + i], self.recv.at[self.base + i], device
            )

        def begin(self):
            for half in (0, 1):
                self.copy(half, self.own(half), self.at, 3, half, self.up).start()
                self.copy(3 + half, self.own(half), self.at, 1, half, self.down).start()

        def forward(self):
            before, after = mod(self.at + 3, 4), mod(self.at + 1, 4)
            self.copy(0, None, before, 3, 0, self.up).wait_recv()
            self.copy(2, self.slot(before, 3, 0), before, 2, 0, self.up).start()
            self.copy(4, None, after, 1, 1, self.down).wait_recv()
            self.copy(5, self.slot(after, 1, 1), after, 2, 1, self.down).start()

        def end(self):
            self.copy(1, None, self.at + 3, 3, 1, self.up).wait_recv()
            self.copy(3, None, self.at + 1, 1, 0, self.down).wait_recv()
            self.copy(2, None, self.at + 2, 2, 0, self.up).wait_recv()
            self.copy(5, None, self.at + 2, 2, 1, self.down).wait_recv()

        def sent(self):
            for i in range(6):
                self.copy(i, None, self.at + 2, 2, (0, 1, 0, 0, 1, 1)[i], self.up).wait_send()

    def y_ring(src, dst, start, size, base):
        return Ring(
            lambda half: src.at[pl.ds(start + half * size, size)],
            lambda origin, rel, half: dst.at[rel - 1, pl.ds(start + half * size, size)],
            y, up_y, down_y, row_send, row_recv, base,
        )

    def x_ring(dst, size, base):
        def slot(origin, rel, half):
            start = core * 8 * size + origin * 2 * size + half * size
            return dst.at[pl.ds(0, 3), pl.ds(pl.multiple_of(start, size), size)]

        return Ring(lambda half: slot(x, 0, half), slot, x, up_x, down_x, col_send, col_recv, base)

    narrow = [
        y_ring(src, dst, pl.multiple_of((core * nx + x) * 2 * size, 2 * size), size, 6 * i)
        for i, (src, dst, size) in enumerate(((wq_ref, wq, 64), (wv_ref, wv, 64), (wo_ref, wo, 16)))
    ]
    wide = y_ring(wk_ref, wk, pl.multiple_of(core * 512, 512), 256, 18)
    across = [x_ring(dst, size, 6 * i) for i, (dst, size) in enumerate(((wq, 64), (wv, 64), (wo, 16)))]

    def slab_slot(origin, rel, half):
        return held_b.at[origin * nc + core, pl.ds(half * 16, 16)]

    beside = Ring(lambda half: slab_slot(x, 0, half), slab_slot, x, up_x, down_x, col_send, col_recv, 18)

    def slab(origin, side):
        ref = held_b.at[origin * nc + side]
        return remote(ref, ref, slab_send.at[origin], slab_recv.at[origin], other)

    def pair(kind, side):
        dst, rows = ((wq, 512), (wk, 512), (wv, 512), (wo, 128))[kind]
        ref = dst.at[pl.ds(0, 3), pl.ds(pl.multiple_of(side * rows, rows), rows)]
        return remote(ref, ref, pair_send.at[kind], pair_recv.at[kind], other)

    for ring in (*narrow, wide):
        ring.begin()

    def turn(q):
        return mod(x + nx - q, nx)

    def hop(way, distance, q, origin):
        ref = held.at[turn(q), pl.ds(pl.multiple_of(origin * part, part), part)]
        i = (way * 4 + distance - 1) * nx + q
        return remote(ref, ref, ring_send.at[i], ring_recv.at[i], (up_z, down_z)[way])

    def origin_of(way, distance):
        return mod(z + nz - distance, nz) if way == 0 else mod(z + distance, nz)

    def goes(way, distance, q):
        return distance < 4 or (q < nx // 2) == (way == 0)

    def ring_begin(q):
        for way in (0, 1):
            hop(way, 1, q, z).start()

    def ring_step(distance):
        for q in range(nx):
            for way in (0, 1):
                if goes(way, distance, q):
                    hop(way, distance, q, origin_of(way, distance)).wait_recv()
                    if distance < 4 and goes(way, distance + 1, q):
                        hop(way, distance + 1, q, origin_of(way, distance)).start()

    def spot(half, s):
        return listed.at[
            half, :,
            pl.ds(pl.multiple_of((over(s, part)) * 16, 16), 16),
            pl.ds(pl.multiple_of((mod(s, part)) * 128, 128), 128),
        ]

    def out(half, t, s):
        i = half * members
        return remote(
            outgoing.at[half, t], spot(half, s), out_send.at[i + t], out_recv.at[i + s], member(half, t)
        )

    def pick(half, t):
        row = (over(t, part) * nz + z) * part + mod(t, part) if half == 0 else (x * nz + over(t, ny)) * part + core * ny + mod(t, ny)
        for e in range(LIST_LEN):
            view, block = views[e, row], blocks[e, row]
            if half == 0:
                outgoing[half, t, e] = held[over(view, 16), mod(view, 16) * ny + block]
            else:
                outgoing[half, t, e] = held_b[over(view, 16) * nc + mod(view, 2), over(mod(view, 16), 2) * ny + block]

    def deal(half, first, last):
        me = places[half]

        def start(k, carry):
            t = mod(me + k * STRIDE, members)
            pick(half, t)
            out(half, t, me).start()
            return carry

        lax.fori_loop(first, last, start, 0)

    def keep(half):
        me = places[half]
        pick(half, me)
        copy = pltpu.make_async_copy(outgoing.at[half, me], spot(half, me), own_sem.at[9 + half])
        copy.start()
        return copy

    def pre_wait(half, first, last):
        def wait(s, carry):
            @pl.when(s != places[half])
            def _():
                pre(half, s, s).wait_recv()
            return carry

        lax.fori_loop(first, last, wait, 0)

    pre_wait(1, 0, members)
    beside.begin()
    slab(x, core).start()
    for q in range(nx):
        pre_wait(0, turn(q) * part, turn(q) * part + part)
        ring_begin(q)
    for copy in lists:
        copy.wait()

    beside.forward()
    ring_step(1)
    for ring in narrow:
        ring.forward()
    beside.end()
    for i in range(1, nx):
        slab(mod(x + i, nx), core).start()
    ring_step(2)
    wide.forward()
    for ring, far in zip(narrow, across):
        ring.end()
        far.begin()
    for i in range(nx):
        slab(mod(x + i, nx), 1 - core).wait_recv()
    deal(1, 1, 16)
    ring_step(3)
    deal(1, 16, members)
    late = keep(1)
    for ring in across:
        ring.forward()
    ring_step(4)
    wide.end()
    pair(1, core).start()
    deal(0, 1, 16)
    for kind, ring in zip((0, 2), across):
        ring.end()
        pair(kind, core).start()
    deal(0, 16, members)
    local = [keep(0), late]
    across[2].end()
    pair(3, core).start()

    for copy in mine:
        copy.wait()
    pair(0, 1 - core).wait_recv()
    wide_cols = D // ny
    group_heads = wide_cols // HEAD_DIM
    lane_head = over(lax.broadcasted_iota(jnp.int32, (1, wide_cols), 1), HEAD_DIM)
    aim = normalize(target[...])
    for g in range(ny):
        query = jnp.dot(aim, wq[g], preferred_element_type=jnp.float32)
        for h in range(group_heads):
            split[g, h * BLOCK:(h + 1) * BLOCK] = jnp.where(lane_head == h, query, 0.0).astype(jnp.bfloat16)
    for kind in (1, 2):
        pair(kind, 1 - core).wait_recv()

    span = LIST_LEN * HALF_ROWS
    columns = lax.broadcasted_iota(jnp.int32, (1, span), 1)
    shade = jnp.where(columns < counts_ref[y] * HALF_ROWS, 0.0, -1e30)
    stretch = HEAD_DIM ** (-0.5) * LOG2E

    def arrive(half):
        def wait(k, carry):
            s = mod(places[half] + k, members)
            out(half, s, s).wait_recv()
            return carry

        lax.fori_loop(1, members, wait, 0)
        local[half].wait()

    def project(half):
        rows = listed[half].reshape(span, D)
        at = slice(half * span, (half + 1) * span)
        for g in range(ny):
            key = jnp.dot(rows, wk[g], preferred_element_type=jnp.float32).astype(jnp.bfloat16)
            values[g, at] = jnp.dot(rows, wv[g], preferred_element_type=jnp.float32).astype(jnp.bfloat16)
            scores[g, :, at] = lax.dot_general(
                split[g], key, (((1,), (1,)), ((), ())), preferred_element_type=jnp.float32
            )

    per_group = group_heads * BLOCK // CHUNK

    def chunk_at(i):
        return over(i, per_group), pl.ds(pl.multiple_of(mod(i, per_group) * CHUNK, CHUNK), CHUNK)

    def soften(i, carry):
        g, rows = chunk_at(i)
        logits = scores[g, rows, span:2 * span] + shade
        peak = jnp.max(logits, axis=1, keepdims=True)
        weights = jnp.exp2((logits - peak) * stretch)
        scores[g, rows, span:2 * span] = weights
        peaks[g, rows] = jnp.broadcast_to(peak, (CHUNK, 128))
        sums[g, rows] = jnp.broadcast_to(jnp.sum(weights, axis=1, keepdims=True), (CHUNK, 128))
        return carry

    def finish(g, rows):
        logits = scores[g, rows, 0:span] + shade
        before = peaks[g, rows][:, 0:1]
        peak = jnp.maximum(before, jnp.max(logits, axis=1, keepdims=True))
        weights = jnp.exp2((logits - peak) * stretch)
        fade = jnp.exp2((before - peak) * stretch)
        whole = fade * sums[g, rows][:, 0:1] + jnp.sum(weights, axis=1, keepdims=True)
        share = 1.0 / whole
        probs[g, rows, 0:span] = (weights * share).astype(jnp.bfloat16)
        probs[g, rows, span:2 * span] = (scores[g, rows, span:2 * span] * (fade * share)).astype(jnp.bfloat16)

    arrive(1)
    project(1)
    lax.fori_loop(0, ny * per_group, soften, 0)
    arrive(0)
    project(0)
    pair(3, 1 - core).wait_recv()
    mixed = jnp.zeros((BLOCK, D), jnp.float32)
    for g in range(ny):
        for h in range(group_heads):
            finish(g, slice(h * BLOCK, (h + 1) * BLOCK))
        summed = jnp.dot(probs[g], values[g], preferred_element_type=jnp.float32)
        attended = jnp.zeros((BLOCK, wide_cols), jnp.float32)
        for h in range(group_heads):
            attended = jnp.where(lane_head == h, summed[h * BLOCK:(h + 1) * BLOCK], attended)
        mixed += jnp.dot(attended.astype(jnp.bfloat16), wo[g], preferred_element_type=jnp.float32)
    total[...] = (target[...].astype(jnp.float32) + mixed).astype(jnp.bfloat16)
    deliver = pltpu.make_async_copy(total, result_ref, own_sem.at[8])
    deliver.start()

    def drain(k, carry):
        for half in range(HALVES):
            t = mod(places[half] + k, members)
            pre(half, t, places[half]).wait_send()
            out(half, t, places[half]).wait_send()
        return carry

    lax.fori_loop(1, members, drain, 0)
    for way in (0, 1):
        for distance in range(1, 5):
            for q in range(nx):
                if goes(way, distance, q):
                    hop(way, distance, q, z).wait_send()
    for ring in (*narrow, wide, *across, beside):
        ring.sent()
    for i in range(nx):
        slab(mod(x + i, nx), core).wait_send()
    for kind in range(4):
        pair(kind, core).wait_send()
    deliver.wait()


def body(target_tokens, input_tokens, w_query, w_key, w_value, w_out, table, table_block, counts):
    members = 32
    cols = D // PIX
    smem, hbm = pl.BlockSpec(memory_space=pltpu.SMEM), pl.BlockSpec(memory_space=pltpu.HBM)
    dma = pltpu.SemaphoreType.DMA
    tall = pltpu.VMEM((PIX, D, cols), jnp.bfloat16)
    block = pltpu.VMEM((BLOCK, D), jnp.bfloat16)
    listed_rows = LIST_LEN * BLOCK
    stats = pltpu.VMEM((PIX, 4 * BLOCK, 128), jnp.float32)
    return pl.pallas_call(
        kernel,
        out_shape=jax.ShapeDtypeStruct((BLOCK, D), jnp.bfloat16),
        in_specs=[hbm, hbm, smem] + [hbm] * 6,
        out_specs=hbm,
        scratch_shapes=[
            pltpu.VMEM((HALVES, LIST_LEN, HALF_ROWS, D), jnp.bfloat16),
            tall, tall, tall,
            pltpu.VMEM((PIX, cols, D), jnp.bfloat16),
            block, block,
            pltpu.VMEM((members, HALVES, 16, 128), jnp.bfloat16),
            pltpu.VMEM((4, 64, 16, 128), jnp.bfloat16),
            pltpu.VMEM((8, 32, 16, 128), jnp.bfloat16),
            pltpu.VMEM((HALVES, members, LIST_LEN, 16, 128), jnp.bfloat16),
            pltpu.VMEM((PIX, 4 * BLOCK, cols), jnp.bfloat16),
            pltpu.VMEM((PIX, listed_rows, cols), jnp.bfloat16),
            pltpu.VMEM((PIX, 4 * BLOCK, listed_rows), jnp.float32),
            pltpu.VMEM((PIX, 4 * BLOCK, listed_rows), jnp.bfloat16),
            stats, stats,
            block,
            pltpu.SMEM((LIST_LEN, 8 * members), jnp.int32),
            pltpu.SMEM((LIST_LEN, 8 * members), jnp.int32),
            dma((HALVES * members,)), dma((HALVES * members,)),
            dma((32,)), dma((32,)),
            dma((HALVES * members,)), dma((HALVES * members,)),
            dma((24,)), dma((24,)),
            dma((24,)), dma((24,)),
            dma((4,)), dma((4,)),
            dma((4,)), dma((4,)),
            dma((9 + HALVES,)),
        ],
        compiler_params=pltpu.CompilerParams(
            collective_id=0, has_side_effects=True, vmem_limit_bytes=60 * 1024 * 1024
        ),
        cost_estimate=pl.CostEstimate(flops=5_400_000_000, bytes_accessed=3 << 20, transcendentals=2 << 20),
    )(table.T, table_block.T, counts, target_tokens, input_tokens, w_query, w_key, w_value, w_out)


def solution(mesh):
    views = ("x", "z", "core")
    fine = Mesh(mesh.devices.reshape(4, 8, 2, 4), ("x", "z", "core", "pix"))
    placed = (
        P((*views, "pix"), None),
        P((*views, "pix"), None),
        P(None, "pix"),
        P(None, "pix"),
        P(None, "pix"),
        P("pix", None),
        P(),
        P(),
        P(views),
    )
    return jax.shard_map(
        body, mesh=fine, in_specs=placed, out_specs=P((*views, "pix"), None), check_vma=False
    )
```

```python
import jax
import jax.numpy as jnp
from jax import lax
from jax.experimental import pallas as pl
from jax.experimental.pallas import tpu as pltpu
from jax.sharding import Mesh, PartitionSpec as P

D = 1024
HEAD_DIM = 64
BLOCK = 128
LIST_LEN = 8
PIX = 4
HALVES = 2
STRIDE = 11
HALF_ROWS = BLOCK // HALVES
CHUNK = 256
LOG2E = 1.4426950408889634


def normalize(tokens):
    source = tokens.astype(jnp.float32)
    center = source - jnp.mean(source, axis=1, keepdims=True)
    spread = jnp.mean(center * center, axis=1, keepdims=True)
    return (center * lax.rsqrt(spread + 1e-05)).astype(jnp.bfloat16)


def mod(value, power):
    return value % power if isinstance(value, int) else value & (power - 1)


def over(value, power):
    return value // power if isinstance(value, int) else value >> (power.bit_length() - 1)


def kernel(
    table_ref, block_ref, counts_ref, target_ref, tokens_ref, wq_ref, wk_ref, wv_ref, wo_ref,
    result_ref,
    listed, wq, wk, wv, wo, target, tokens, pieces, held, held_b, outgoing,
    split, values, scores, probs, peaks, sums, total, views, blocks,
    pre_send, pre_recv, ring_send, ring_recv, out_send, out_recv,
    row_send, row_recv, col_send, col_recv, slab_send, slab_recv, pair_send, pair_recv, own_sem,
):
    x, z, core, y = (lax.axis_index(name) for name in ("x", "z", "core", "pix"))
    nx, nz, nc, ny = (lax.axis_size(name) for name in ("x", "z", "core", "pix"))
    part = nc * ny
    members = nx * part
    places = (x * part + core * ny + y, z * ny + y)

    def member(half, t):
        if half == 0:
            return (over(t, part), z, mod(over(t, ny), nc), mod(t, ny))
        return (x, over(t, ny), core, mod(t, ny))

    up_z, down_z = (x, mod(z + 1, nz), core, y), (x, mod(z + nz - 1, nz), core, y)
    up_y, down_y = (x, z, core, mod(y + 1, ny)), (x, z, core, mod(y + ny - 1, ny))
    up_x, down_x = (mod(x + 1, nx), z, core, y), (mod(x + nx - 1, nx), z, core, y)
    other = (x, z, 1 - core, y)

    def remote(src, dst, send, recv, device):
        return pltpu.make_async_remote_copy(
            src_ref=src, dst_ref=dst, send_sem=send, recv_sem=recv,
            device_id=device, device_id_type=pl.DeviceIdType.MESH,
        )

    fetch = pltpu.make_async_copy(tokens_ref, tokens, own_sem.at[0])
    fetch.start()
    barrier = pltpu.get_barrier_semaphore()

    def greet(k, carry):
        for half in range(HALVES):
            pl.semaphore_signal(
                barrier, inc=1, device_id=member(half, mod(places[half] + k, members)),
                device_id_type=pl.DeviceIdType.MESH,
            )
        return carry

    for k in range(1, members):
        greet(k, 0)
    lists = [
        pltpu.make_async_copy(src, dst, own_sem.at[1 + i])
        for i, (src, dst) in enumerate(((table_ref, views), (block_ref, blocks)))
    ]
    mine = [
        pltpu.make_async_copy(src, dst, own_sem.at[3 + i])
        for i, (src, dst) in enumerate(
            ((wq_ref, wq.at[ny - 1]), (wk_ref, wk.at[ny - 1]), (wv_ref, wv.at[ny - 1]), (wo_ref, wo.at[ny - 1]), (target_ref, target))
        )
    ]
    for copy in lists + mine:
        copy.start()
    fetch.wait()
    normed = normalize(tokens[...])
    for t in range(members):
        for half in range(HALVES):
            top, left = half * HALF_ROWS + (over(t, part)) * 16, (mod(t, part)) * 128
            pieces[t, half] = normed[top:top + 16, left:left + 128]
    held[x, z * part + core * ny + y] = pieces[places[0], 0]
    held_b[x * nc + core, places[1]] = pieces[places[1], 1]
    pl.semaphore_wait(barrier, HALVES * (members - 1))

    def pre(half, t, s):
        dst = held.at[over(s, part), z * part + mod(s, part)] if half == 0 else held_b.at[x * nc + core, s]
        i = half * members
        return remote(pieces.at[t, half], dst, pre_send.at[i + t], pre_recv.at[i + s], member(half, t))

    def pre_start(k, carry):
        for half in (1, 0):
            pre(half, mod(places[half] + k, members), places[half]).start()
        return carry

    for k in range(1, members):
        pre_start(k, 0)

    class Ring:
        def __init__(self, own, slot, at, up, down, send, recv, base):
            self.own, self.slot, self.at, self.up, self.down = own, slot, at, up, down
            self.send, self.recv, self.base = send, recv, base

        def copy(self, i, src, origin, rel, half, device):
            dst = self.slot(mod(origin, 4), rel, half)
            return remote(
                dst if src is None else src, dst, self.send.at[self.base + i], self.recv.at[self.base + i], device
            )

        def begin(self):
            for half in (0, 1):
                self.copy(half, self.own(half), self.at, 3, half, self.up).start()
                self.copy(3 + half, self.own(half), self.at, 1, half, self.down).start()

        def forward(self):
            before, after = mod(self.at + 3, 4), mod(self.at + 1, 4)
            self.copy(0, None, before, 3, 0, self.up).wait_recv()
            self.copy(2, self.slot(before, 3, 0), before, 2, 0, self.up).start()
            self.copy(4, None, after, 1, 1, self.down).wait_recv()
            self.copy(5, self.slot(after, 1, 1), after, 2, 1, self.down).start()

        def end(self):
            self.copy(1, None, self.at + 3, 3, 1, self.up).wait_recv()
            self.copy(3, None, self.at + 1, 1, 0, self.down).wait_recv()
            self.copy(2, None, self.at + 2, 2, 0, self.up).wait_recv()
            self.copy(5, None, self.at + 2, 2, 1, self.down).wait_recv()

        def sent(self):
            for i in range(6):
                self.copy(i, None, self.at + 2, 2, (0, 1, 0, 0, 1, 1)[i], self.up).wait_send()

    def y_ring(src, dst, start, size, base):
        return Ring(
            lambda half: src.at[pl.ds(start + half * size, size)],
            lambda origin, rel, half: dst.at[rel - 1, pl.ds(start + half * size, size)],
            y, up_y, down_y, row_send, row_recv, base,
        )

    def x_ring(dst, size, base):
        def slot(origin, rel, half):
            start = core * 8 * size + origin * 2 * size + half * size
            return dst.at[pl.ds(0, 3), pl.ds(pl.multiple_of(start, size), size)]

        return Ring(lambda half: slot(x, 0, half), slot, x, up_x, down_x, col_send, col_recv, base)

    narrow = [
        y_ring(src, dst, pl.multiple_of((core * nx + x) * 2 * size, 2 * size), size, 6 * i)
        for i, (src, dst, size) in enumerate(((wq_ref, wq, 64), (wv_ref, wv, 64), (wo_ref, wo, 16)))
    ]
    wide = y_ring(wk_ref, wk, pl.multiple_of(core * 512, 512), 256, 18)
    across = [x_ring(dst, size, 6 * i) for i, (dst, size) in enumerate(((wq, 64), (wv, 64), (wo, 16)))]

    def slab_slot(origin, rel, half):
        return held_b.at[origin * nc + core, pl.ds(half * 16, 16)]

    beside = Ring(lambda half: slab_slot(x, 0, half), slab_slot, x, up_x, down_x, col_send, col_recv, 18)

    def slab(origin, side):
        ref = held_b.at[origin * nc + side]
        return remote(ref, ref, slab_send.at[origin], slab_recv.at[origin], other)

    def pair(kind, side):
        dst, rows = ((wq, 512), (wk, 512), (wv, 512), (wo, 128))[kind]
        ref = dst.at[pl.ds(0, 3), pl.ds(pl.multiple_of(side * rows, rows), rows)]
        return remote(ref, ref, pair_send.at[kind], pair_recv.at[kind], other)

    for ring in (*narrow, wide):
        ring.begin()

    def turn(q):
        return mod(x + nx - q, nx)

    def hop(way, distance, q, origin):
        ref = held.at[turn(q), pl.ds(pl.multiple_of(origin * part, part), part)]
        i = (way * 4 + distance - 1) * nx + q
        return remote(ref, ref, ring_send.at[i], ring_recv.at[i], (up_z, down_z)[way])

    def origin_of(way, distance):
        return mod(z + nz - distance, nz) if way == 0 else mod(z + distance, nz)

    def goes(way, distance, q):
        return distance < 4 or (q < nx // 2) == (way == 0)

    def ring_begin(q):
        for way in (0, 1):
            hop(way, 1, q, z).start()

    def ring_step(distance):
        for q in range(nx):
            for way in (0, 1):
                if goes(way, distance, q):
                    hop(way, distance, q, origin_of(way, distance)).wait_recv()
                    if distance < 4 and goes(way, distance + 1, q):
                        hop(way, distance + 1, q, origin_of(way, distance)).start()

    def spot(half, s):
        return listed.at[
            half, :,
            pl.ds(pl.multiple_of((over(s, part)) * 16, 16), 16),
            pl.ds(pl.multiple_of((mod(s, part)) * 128, 128), 128),
        ]

    def out(half, t, s):
        i = half * members
        return remote(
            outgoing.at[half, t], spot(half, s), out_send.at[i + t], out_recv.at[i + s], member(half, t)
        )

    def pick(half, t):
        row = (over(t, part) * nz + z) * part + mod(t, part) if half == 0 else (x * nz + over(t, ny)) * part + core * ny + mod(t, ny)
        for e in range(LIST_LEN):
            view, block = views[e, row], blocks[e, row]
            if half == 0:
                outgoing[half, t, e] = held[over(view, 16), mod(view, 16) * ny + block]
            else:
                outgoing[half, t, e] = held_b[over(view, 16) * nc + mod(view, 2), over(mod(view, 16), 2) * ny + block]

    def deal(half, first, last):
        me = places[half]

        def start(k, carry):
            if half == 1:
                t = mod(me + k * STRIDE, members)
            elif last < members:
                t = mod(me + 24 + mod(8 + 5 * k, 16), members)
            else:
                t = mod(me + 8 + mod(5 * k, 16), members)
            pick(half, t)
            out(half, t, me).start()
            return carry

        lax.fori_loop(first, last, start, 0)

    def keep(half):
        me = places[half]
        pick(half, me)
        copy = pltpu.make_async_copy(outgoing.at[half, me], spot(half, me), own_sem.at[9 + half])
        copy.start()
        return copy

    def pre_wait(half, first, last):
        def wait(s, carry):
            @pl.when(s != places[half])
            def _():
                pre(half, s, s).wait_recv()
            return carry

        lax.fori_loop(first, last, wait, 0)

    pre_wait(1, 0, members)
    beside.begin()
    slab(x, core).start()
    for q in range(nx):
        pre_wait(0, turn(q) * part, turn(q) * part + part)
        ring_begin(q)
    for copy in lists:
        copy.wait()

    beside.forward()
    ring_step(1)
    for ring in narrow:
        ring.forward()
    beside.end()
    for i in range(1, nx):
        slab(mod(x + i, nx), core).start()
    ring_step(2)
    wide.forward()
    for ring, far in zip(narrow, across):
        ring.end()
        far.begin()
    for i in range(nx):
        slab(mod(x + i, nx), 1 - core).wait_recv()
    deal(1, 1, 16)
    ring_step(3)
    deal(1, 16, members)
    late = keep(1)
    for ring in across:
        ring.forward()
    ring_step(4)
    wide.end()
    pair(1, core).start()
    deal(0, 1, 16)
    for kind, ring in zip((0, 2), across):
        ring.end()
        pair(kind, core).start()
    deal(0, 16, members)
    local = [keep(0), late]
    across[2].end()
    pair(3, core).start()

    for copy in mine:
        copy.wait()
    pair(0, 1 - core).wait_recv()
    wide_cols = D // ny
    group_heads = wide_cols // HEAD_DIM
    lane_head = over(lax.broadcasted_iota(jnp.int32, (1, wide_cols), 1), HEAD_DIM)
    aim = normalize(target[...])
    for g in range(ny):
        query = jnp.dot(aim, wq[g], preferred_element_type=jnp.float32)
        for h in range(group_heads):
            split[g, h * BLOCK:(h + 1) * BLOCK] = jnp.where(lane_head == h, query, 0.0).astype(jnp.bfloat16)
    for kind in (1, 2):
        pair(kind, 1 - core).wait_recv()

    span = LIST_LEN * HALF_ROWS
    columns = lax.broadcasted_iota(jnp.int32, (1, span), 1)
    shade = jnp.where(columns < counts_ref[y] * HALF_ROWS, 0.0, -1e30)
    fine_shade = jnp.where(mod(columns, LIST_LEN * 16) < counts_ref[y] * 16, 0.0, -1e30)
    stretch = HEAD_DIM ** (-0.5) * LOG2E

    def arrive(half):
        def wait(k, carry):
            s = mod(places[half] + k, members)
            out(half, s, s).wait_recv()
            return carry

        lax.fori_loop(1, members, wait, 0)
        local[half].wait()

    def absorb(rows, at):
        for g in range(ny):
            key = jnp.dot(rows, wk[g], preferred_element_type=jnp.float32).astype(jnp.bfloat16)
            values[g, at] = jnp.dot(rows, wv[g], preferred_element_type=jnp.float32).astype(jnp.bfloat16)
            scores[g, :, at] = lax.dot_general(
                split[g], key, (((1,), (1,)), ((), ())), preferred_element_type=jnp.float32
            )

    per_group = group_heads * BLOCK // CHUNK

    def chunk_at(i):
        return over(i, per_group), pl.ds(pl.multiple_of(mod(i, per_group) * CHUNK, CHUNK), CHUNK)

    def soften(i, carry):
        g, rows = chunk_at(i)
        logits = scores[g, rows, span:2 * span] + shade
        peak = jnp.max(logits, axis=1, keepdims=True)
        weights = jnp.exp2((logits - peak) * stretch)
        scores[g, rows, span:2 * span] = weights
        peaks[g, rows] = jnp.broadcast_to(peak, (CHUNK, 128))
        sums[g, rows] = jnp.broadcast_to(jnp.sum(weights, axis=1, keepdims=True), (CHUNK, 128))
        return carry

    def finish(g, rows):
        logits = scores[g, rows, 0:span] + fine_shade
        before = peaks[g, rows][:, 0:1]
        peak = jnp.maximum(before, jnp.max(logits, axis=1, keepdims=True))
        weights = jnp.exp2((logits - peak) * stretch)
        fade = jnp.exp2((before - peak) * stretch)
        whole = fade * sums[g, rows][:, 0:1] + jnp.sum(weights, axis=1, keepdims=True)
        share = 1.0 / whole
        probs[g, rows, 0:span] = (weights * share).astype(jnp.bfloat16)
        probs[g, rows, span:2 * span] = (scores[g, rows, span:2 * span] * (fade * share)).astype(jnp.bfloat16)

    arrive(1)
    absorb(listed[1].reshape(span, D), slice(span, 2 * span))
    lax.fori_loop(0, ny * per_group, soften, 0)
    for late in range(2):
        for i in (2 * late, 2 * late + 1):
            first = mod(x + i, nx) * part

            def wait(s, carry):
                @pl.when(s != places[0])
                def _():
                    out(0, s, s).wait_recv()
                return carry

            lax.fori_loop(first, first + part, wait, 0)
        if late == 0:
            local[0].wait()
        rows = jnp.concatenate(
            [
                listed[0, :, pl.ds(pl.multiple_of(mod(x + i, nx) * 16, 16), 16)].reshape(LIST_LEN * 16, D)
                for i in (2 * late, 2 * late + 1)
            ],
            axis=0,
        )
        absorb(rows, slice(late * span // 2, (late + 1) * span // 2))
    pair(3, 1 - core).wait_recv()
    mixed = jnp.zeros((BLOCK, D), jnp.float32)
    for g in range(ny):
        for h in range(group_heads):
            finish(g, slice(h * BLOCK, (h + 1) * BLOCK))
        summed = jnp.dot(probs[g], values[g], preferred_element_type=jnp.float32)
        attended = jnp.zeros((BLOCK, wide_cols), jnp.float32)
        for h in range(group_heads):
            attended = jnp.where(lane_head == h, summed[h * BLOCK:(h + 1) * BLOCK], attended)
        mixed += jnp.dot(attended.astype(jnp.bfloat16), wo[g], preferred_element_type=jnp.float32)
    total[...] = (target[...].astype(jnp.float32) + mixed).astype(jnp.bfloat16)
    deliver = pltpu.make_async_copy(total, result_ref, own_sem.at[8])
    deliver.start()

    def drain(k, carry):
        for half in range(HALVES):
            t = mod(places[half] + k, members)
            pre(half, t, places[half]).wait_send()
            out(half, t, places[half]).wait_send()
        return carry

    lax.fori_loop(1, members, drain, 0)
    for way in (0, 1):
        for distance in range(1, 5):
            for q in range(nx):
                if goes(way, distance, q):
                    hop(way, distance, q, z).wait_send()
    for ring in (*narrow, wide, *across, beside):
        ring.sent()
    for i in range(nx):
        slab(mod(x + i, nx), core).wait_send()
    for kind in range(4):
        pair(kind, core).wait_send()
    deliver.wait()


def body(target_tokens, input_tokens, w_query, w_key, w_value, w_out, table, table_block, counts):
    members = 32
    cols = D // PIX
    smem, hbm = pl.BlockSpec(memory_space=pltpu.SMEM), pl.BlockSpec(memory_space=pltpu.HBM)
    dma = pltpu.SemaphoreType.DMA
    tall = pltpu.VMEM((PIX, D, cols), jnp.bfloat16)
    block = pltpu.VMEM((BLOCK, D), jnp.bfloat16)
    listed_rows = LIST_LEN * BLOCK
    stats = pltpu.VMEM((PIX, 4 * BLOCK, 128), jnp.float32)
    return pl.pallas_call(
        kernel,
        out_shape=jax.ShapeDtypeStruct((BLOCK, D), jnp.bfloat16),
        in_specs=[hbm, hbm, smem] + [hbm] * 6,
        out_specs=hbm,
        scratch_shapes=[
            pltpu.VMEM((HALVES, LIST_LEN, HALF_ROWS, D), jnp.bfloat16),
            tall, tall, tall,
            pltpu.VMEM((PIX, cols, D), jnp.bfloat16),
            block, block,
            pltpu.VMEM((members, HALVES, 16, 128), jnp.bfloat16),
            pltpu.VMEM((4, 64, 16, 128), jnp.bfloat16),
            pltpu.VMEM((8, 32, 16, 128), jnp.bfloat16),
            pltpu.VMEM((HALVES, members, LIST_LEN, 16, 128), jnp.bfloat16),
            pltpu.VMEM((PIX, 4 * BLOCK, cols), jnp.bfloat16),
            pltpu.VMEM((PIX, listed_rows, cols), jnp.bfloat16),
            pltpu.VMEM((PIX, 4 * BLOCK, listed_rows), jnp.float32),
            pltpu.VMEM((PIX, 4 * BLOCK, listed_rows), jnp.bfloat16),
            stats, stats,
            block,
            pltpu.SMEM((LIST_LEN, 8 * members), jnp.int32),
            pltpu.SMEM((LIST_LEN, 8 * members), jnp.int32),
            dma((HALVES * members,)), dma((HALVES * members,)),
            dma((32,)), dma((32,)),
            dma((HALVES * members,)), dma((HALVES * members,)),
            dma((24,)), dma((24,)),
            dma((24,)), dma((24,)),
            dma((4,)), dma((4,)),
            dma((4,)), dma((4,)),
            dma((9 + HALVES,)),
        ],
        compiler_params=pltpu.CompilerParams(
            collective_id=0, has_side_effects=True, vmem_limit_bytes=60 * 1024 * 1024
        ),
        cost_estimate=pl.CostEstimate(flops=5_400_000_000, bytes_accessed=3 << 20, transcendentals=2 << 20),
    )(table.T, table_block.T, counts, target_tokens, input_tokens, w_query, w_key, w_value, w_out)


def solution(mesh):
    views = ("x", "z", "core")
    fine = Mesh(mesh.devices.reshape(4, 8, 2, 4), ("x", "z", "core", "pix"))
    placed = (
        P((*views, "pix"), None),
        P((*views, "pix"), None),
        P(None, "pix"),
        P(None, "pix"),
        P(None, "pix"),
        P("pix", None),
        P(),
        P(),
        P(views),
    )
    return jax.shard_map(
        body, mesh=fine, in_specs=placed, out_specs=P((*views, "pix"), None), check_vma=False
    )
```
